512 devices in a mesh: img: 16 (over z_lo, x, core), txt: 32 (over y, z_hi).
Axes of the slice: x: 4, y: 8, z: 8 (z_hi: 4, z_lo: 2; z = z_hi * 2 + z_lo), core: 2. Of those that a mesh axis runs over, the one named last changes fastest.
Arguments:
- image_emb: bfloat16 [16384, 1152], P(('txt', 'img')), may hold values from -6 to 6
- text_emb: bfloat16 [16384, 1152], P(('img', 'txt')), may hold values from -6 to 6
- logit_scale: float32 [1], replicated, may hold values from 10 to 40
- logit_bias: float32 [1], replicated, may hold values from -6 to -3
Outputs:
- grad_image: float32 [16384, 1152], P(('txt', 'img'))
- grad_text: float32 [16384, 1152], P(('img', 'txt'))
The draws below stay inside these ranges and needn't reach their ends.
All inputs are finite; a program needn't handle non-finite values.
Results may differ from the reference program's by a relative error of at most 0.007.
Values may be sent and summed in bfloat16 or wider, within the bound.
No kernel may reach another device: no remote copies, remote signals or barrier semaphores. Data moves between devices by JAX's collectives and lax.ppermute only.
A program may use at most 64 MiB of HBM per device.

```python
import math
import jax
import jax.numpy as jnp
from jax import lax

D = 1152
PAIRS = 16384


def block_levels(key, extent, shards, least, largest):
    loudness, own = 1.0, jax.random.fold_in(key, 6)
    for position, shards_of in shards:
        draws = jnp.exp(jax.random.uniform(jax.random.fold_in(own, position), (shards_of,), jnp.float32, least / len(shards), largest / len(shards)))
        loudness = loudness * jnp.repeat(draws, extent[position] // shards_of).reshape([-1 if axis == position else 1 for axis in range(len(extent))])
    return loudness


def noise(rng, dims, scale, most, pieces=(), kind=jnp.bfloat16):
    array = jax.random.normal(rng, dims, jnp.float32) * scale
    if len(pieces) > 0:
        array = block_levels(rng, dims, pieces, -0.22, 0.18) * array
    return jnp.clip(array, min=-most, max=most).astype(kind)


def setup_inputs(seed: int = 0) -> dict:
    key_of = jax.random.split(jax.random.key(seed), 5)
    return {
        "image_emb": noise(key_of[0], (PAIRS, D), 1.0, 6.0, ((0, 512),)),
        "text_emb": noise(key_of[1], (PAIRS, D), 1.0, 6.0, ((0, 512),)),
        "logit_scale": jnp.clip(jnp.exp(jax.random.uniform(key_of[2], (1,), jnp.float32, math.log(10.0), math.log(40.0))), 10.0, 40.0),
        "logit_bias": jnp.clip(jax.random.uniform(key_of[3], (1,), jnp.float32, -6.0, -3.0), -6.0, -3.0),
    }


EPS = 1e-06

def unit_rows(embedded):
    values = embedded.astype(jnp.float32)
    inverse = lax.rsqrt(lax.optimization_barrier(jnp.sum(values * values, axis=1, keepdims=True)) + EPS)
    return (values * inverse, inverse)

def project_back(grad, unit, inverse):
    inner = lax.optimization_barrier(jnp.sum(unit * grad, axis=1, keepdims=True))
    return (grad - unit * inner) * inverse

def reference(image_emb, text_emb, logit_scale, logit_bias):
    scale = logit_scale[0]
    bias = logit_bias[0]
    img_unit, img_inv = unit_rows(image_emb)
    txt_unit, txt_inv = unit_rows(text_emb)
    img_wide = lax.optimization_barrier(img_unit.astype(jnp.bfloat16)).astype(jnp.float32)
    txt_wide = lax.optimization_barrier(txt_unit.astype(jnp.bfloat16)).astype(jnp.float32)
    block = math.gcd(PAIRS, 512)
    count = PAIRS // block
    columns = lax.iota(jnp.int32, PAIRS)

    def one_block(img_sum, index):
        start = (index * block).astype(jnp.int32)
        text_rows = lax.dynamic_slice_in_dim(txt_wide, start, block, 0)
        scores = scale * jnp.dot(text_rows, img_wide.T, preferred_element_type=jnp.float32) + bias
        row_ids = start + lax.iota(jnp.int32, block)
        match = (row_ids[:, None] == columns[None, :]).astype(jnp.float32)
        rounded = lax.optimization_barrier((jax.nn.sigmoid(scores) - match).astype(jnp.bfloat16))
        weights = rounded.astype(jnp.float32)
        txt_grad = scale * jnp.dot(weights, img_wide, preferred_element_type=jnp.float32)
        img_sum = img_sum + scale * jnp.dot(weights.T, text_rows, preferred_element_type=jnp.float32)
        return (img_sum, txt_grad)
    img_grad, txt_blocks = lax.scan(one_block, jnp.zeros((PAIRS, D), jnp.float32), jnp.arange(count, dtype=jnp.int32))
    txt_grad = txt_blocks.reshape(PAIRS, D)
    return (project_back(img_grad, img_unit, img_inv), project_back(txt_grad, txt_unit, txt_inv))
```

```python
import jax
import jax.numpy as jnp
from jax import lax
from jax.sharding import Mesh, PartitionSpec as P

EPS = 1e-06
SIZES = (("zl", 2), ("x", 4), ("c", 2), ("y", 8), ("zh", 4))
IMG_ORDER = ("y", "zh", "zl", "x", "c")
TXT_ORDER = ("zl", "x", "c", "y", "zh")
IMG_GROUP = ("zh", "x")
TXT_GROUP = ("zl", "y")


def unit_rows(embedded):
    values = embedded.astype(jnp.float32)
    inverse = lax.rsqrt(jnp.sum(values * values, axis=1, keepdims=True) + EPS)
    return (values * inverse, inverse)


def project_back(grad, unit, inverse):
    inner = jnp.sum(unit * grad, axis=1, keepdims=True)
    return (grad - unit * inner) * inverse


def exchange(blocks, axes):
    return lax.all_to_all(blocks, axes, 0, 0, tiled=False)


def spread(rows, axes):
    count = lax.axis_size(axes)
    copies = lax.optimization_barrier(jnp.broadcast_to(rows[None], (count,) + rows.shape))
    return exchange(copies, axes)


def swap_cores(block):
    return lax.ppermute(block, "c", [(0, 1), (1, 0)])


def row_ids(order, group, rows, fixed):
    size = dict(SIZES)
    count = 1
    for name in group:
        count *= size[name]
    index = lax.iota(jnp.int32, count * rows)
    peer, row = index // rows, index % rows
    place = {}
    for name in reversed(group):
        place[name] = peer % size[name]
        peer = peer // size[name]
    block = jnp.zeros_like(index)
    for name in order:
        block = block * size[name] + place.get(name, fixed[name])
    return block * rows + row


def weigh(text, image, text_ids, image_ids, scale, bias):
    scores = lax.dot_general(text, image, (((1,), (1,)), ((), ())), preferred_element_type=jnp.float32)
    match = (text_ids[:, None] == image_ids[None, :]).astype(jnp.float32)
    return (jax.nn.sigmoid(scale * scores + bias) - match).astype(jnp.bfloat16)


def down(weights, text):
    return lax.dot_general(weights, text, (((0,), (0,)), ((), ())), preferred_element_type=jnp.float32)


def per_device(image_emb, text_emb, logit_scale, logit_bias):
    scale = logit_scale[0]
    bias = logit_bias[0]
    rows, width = image_emb.shape
    img_unit, img_inv = unit_rows(image_emb)
    txt_unit, txt_inv = unit_rows(text_emb)

    own = spread(img_unit.astype(jnp.bfloat16), IMG_GROUP)
    own = own.reshape(-1, width)
    other = swap_cores(own)
    text = spread(txt_unit.astype(jnp.bfloat16), TXT_GROUP).reshape(-1, width)

    here = {name: lax.axis_index(name) for name, _ in SIZES}
    there = dict(here, c=1 - here["c"])
    text_ids = row_ids(TXT_ORDER, TXT_GROUP, rows, here)
    own_ids = row_ids(IMG_ORDER, IMG_GROUP, rows, here)
    other_ids = row_ids(IMG_ORDER, IMG_GROUP, rows, there)

    other_weights = weigh(text, other, text_ids, other_ids, scale, bias)
    foreign = swap_cores(down(other_weights, text).astype(jnp.bfloat16))
    own_weights = weigh(text, own, text_ids, own_ids, scale, bias)
    txt_part = jnp.dot(own_weights, own, preferred_element_type=jnp.float32)
    txt_part = txt_part + jnp.dot(other_weights, other, preferred_element_type=jnp.float32)
    txt_parts = exchange(txt_part.astype(jnp.bfloat16).reshape(-1, rows, width), TXT_GROUP)
    img_part = down(own_weights, text) + foreign.astype(jnp.float32)
    img_parts = exchange(img_part.astype(jnp.bfloat16).reshape(-1, rows, width), IMG_GROUP)

    txt_grad = scale * jnp.sum(txt_parts.astype(jnp.float32), axis=0)
    img_grad = scale * jnp.sum(img_parts.astype(jnp.float32), axis=0)
    return (project_back(img_grad, img_unit, img_inv), project_back(txt_grad, txt_unit, txt_inv))


def solution(mesh):
    names = tuple(name for name, _ in SIZES)
    fine = Mesh(mesh.devices.reshape(tuple(size for _, size in SIZES)), names)
    placed = (P(IMG_ORDER, None), P(TXT_ORDER, None), P(), P())
    return jax.shard_map(
        per_device,
        mesh=fine,
        in_specs=placed,
        out_specs=(P(IMG_ORDER, None), P(TXT_ORDER, None)),
        check_vma=False,
    )
```

```python
import jax
import jax.numpy as jnp
from jax import lax
from jax.experimental import pallas as pl
from jax.experimental.pallas import tpu as pltpu
from jax.sharding import Mesh, PartitionSpec as P

EPS = 1e-06
NAMES = ("zl", "xh", "xl", "c", "y", "zh")
SHAPE = (2, 2, 2, 2, 8, 4)
IMG_ORDER = ("y", "zh", "zl", "xh", "xl", "c")
TXT_ORDER = ("zl", "xh", "xl", "c", "y", "zh")
PEERS = 16
HALF = 2
MIB = 1 << 20


def device_index(x, y, z, c):
    return ((((z % 2) * 4 + x) * 2 + c) * 8 + y) * 4 + z // 2


def exchange_groups():
    text = [
        [device_index(x, y, z, 0) for x in (first, first + 1) for y in range(8)]
        for first in (0, 2)
        for z in range(8)
    ]
    image = [
        [device_index(x, y, z, 1) for x in (first, 3 - first) for z in range(8)]
        for first in (0, 1)
        for y in range(8)
    ]
    return text + image


def exchange(blocks):
    return lax.all_to_all(blocks, NAMES, 0, 0, axis_index_groups=exchange_groups(), tiled=False)


def swap_cores(block):
    return lax.ppermute(block, "c", [(0, 1), (1, 0)])


def unit_rows(embedded):
    values = embedded.astype(jnp.float32)
    inverse = lax.rsqrt(jnp.sum(values * values, axis=1, keepdims=True) + EPS)
    return (values * inverse, inverse)


def project_back(grad, unit, inverse):
    inner = jnp.sum(unit * grad, axis=1, keepdims=True)
    return (grad - unit * inner) * inverse


def normalize_kernel(place, image, text, mine, given):
    img_unit = unit_rows(image[...])[0]
    txt_unit = unit_rows(text[...])[0]
    speaks_text = place[0] == 0
    mine[...] = jnp.where(speaks_text, txt_unit, img_unit).astype(jnp.bfloat16)
    given[...] = jnp.where(speaks_text, img_unit, txt_unit).astype(jnp.bfloat16)


def global_rows(index, is_text, place, rows):
    x, y, zl, zh = place[1], place[2], place[3], place[4]
    row = index % rows
    slot = (index // rows) % 2
    peer = index // (2 * rows)
    side, ring = peer // 8, peer % 8
    text = (((zl * 4 + (x // 2) * 2 + side) * 2 + slot) * 8 + ring) * 4 + zh
    low = jnp.minimum(x, 3 - x)
    across = low + side * (3 - 2 * low)
    image = ((y * 8 + ring) * 4 + across) * 2 + 1 - slot
    return jnp.where(is_text, text, image) * rows + row


def tile_kernel(rows, place, scalars, mine, theirs, grad_mine, grad_theirs):
    core = place[0]
    speaks_text = core == 0
    scale, bias = scalars[0], scalars[1]
    part = mine.shape[0] // HALF
    for half in range(HALF):
        start = pl.multiple_of(((half + core) % HALF) * part, part)
        here = mine[half * part : (half + 1) * part, :]
        there = theirs[pl.ds(start, part), :]
        scores = lax.dot_general(here, there, (((1,), (1,)), ((), ())), preferred_element_type=jnp.float32)
        here_ids = global_rows(
            half * part + lax.broadcasted_iota(jnp.int32, (part, 1), 0), speaks_text, place, rows
        )
        there_ids = global_rows(
            start + lax.broadcasted_iota(jnp.int32, (1, part), 1), jnp.logical_not(speaks_text), place, rows
        )
        match = jnp.where(here_ids == there_ids, 1.0, 0.0)
        weights = (jax.nn.sigmoid(scale * scores + bias) - match).astype(jnp.bfloat16)
        grad_mine[half * part : (half + 1) * part, :] = jnp.dot(
            weights, there, preferred_element_type=jnp.float32
        )
        grad_theirs[pl.ds(start, part), :] = lax.dot_general(
            weights, here, (((0,), (0,)), ((), ())), preferred_element_type=jnp.float32
        ).astype(jnp.bfloat16)


def finish_kernel(place, scalars, summed, received, image, text, grad_image, grad_text):
    speaks_text = place[0] == 0
    scale = scalars[0]
    own, other = scale * summed[...], scale * received[...]
    img_unit, img_inv = unit_rows(image[...])
    txt_unit, txt_inv = unit_rows(text[...])
    grad_image[...] = project_back(jnp.where(speaks_text, other, own), img_unit, img_inv)
    grad_text[...] = project_back(jnp.where(speaks_text, own, other), txt_unit, txt_inv)


SMEM = pl.BlockSpec(memory_space=pltpu.SMEM)
VMEM = pl.BlockSpec(memory_space=pltpu.VMEM)


def per_device(image_emb, text_emb, logit_scale, logit_bias):
    rows, width = image_emb.shape
    x = lax.axis_index("xh") * 2 + lax.axis_index("xl")
    place = jnp.stack(
        [lax.axis_index("c"), x, lax.axis_index("y"), lax.axis_index("zl"), lax.axis_index("zh")]
    ).astype(jnp.int32)
    scalars = jnp.concatenate([logit_scale, logit_bias])

    small = jax.ShapeDtypeStruct((rows, width), jnp.bfloat16)
    mine, given = pl.pallas_call(
        normalize_kernel,
        out_shape=(small, small),
        in_specs=[SMEM, VMEM, VMEM],
        out_specs=(VMEM, VMEM),
        name="normalize",
    )(place, image_emb, text_emb)
    block = jnp.concatenate([mine, swap_cores(given)], axis=0)
    copies = lax.optimization_barrier(jnp.broadcast_to(block[None], (PEERS, 2 * rows, width)))
    mine = exchange(copies).reshape(PEERS * 2 * rows, width)
    theirs = swap_cores(mine)

    total = PEERS * 2 * rows
    grad_mine, grad_theirs = pl.pallas_call(
        lambda *refs: tile_kernel(rows, *refs),
        out_shape=(
            jax.ShapeDtypeStruct((total, width), jnp.float32),
            jax.ShapeDtypeStruct((total, width), jnp.bfloat16),
        ),
        in_specs=[SMEM, SMEM, VMEM, VMEM],
        out_specs=(VMEM, VMEM),
        compiler_params=pltpu.CompilerParams(vmem_limit_bytes=40 * MIB),
        cost_estimate=pl.CostEstimate(
            flops=3 * total * total * width, bytes_accessed=10 * total * width, transcendentals=total * total // 2
        ),
        name="tile",
    )(place, scalars, mine, theirs)

    partial = grad_mine + swap_cores(grad_theirs).astype(jnp.float32)
    parts = exchange(partial.astype(jnp.bfloat16).reshape(PEERS, 2 * rows, width))
    summed = jnp.sum(parts.astype(jnp.float32), axis=0)
    received = swap_cores(summed[rows:])
    out = jax.ShapeDtypeStruct((rows, width), jnp.float32)
    return pl.pallas_call(
        finish_kernel,
        out_shape=(out, out),
        in_specs=[SMEM, SMEM, VMEM, VMEM, VMEM, VMEM],
        out_specs=(VMEM, VMEM),
        name="finish",
    )(place, scalars, summed[:rows], received, image_emb, text_emb)


def solution(mesh):
    fine = Mesh(mesh.devices.reshape(SHAPE), NAMES)
    return jax.shard_map(
        per_device,
        mesh=fine,
        in_specs=(P(IMG_ORDER, None), P(TXT_ORDER, None), P(), P()),
        out_specs=(P(IMG_ORDER, None), P(TXT_ORDER, None)),
        check_vma=False,
    )
```

```python
import jax
import jax.numpy as jnp
from jax import lax
from jax.experimental import pallas as pl
from jax.experimental.pallas import tpu as pltpu
from jax.sharding import Mesh, PartitionSpec as P

EPS = 1e-06
NAMES = ("zl", "xh", "xl", "c", "y", "zh")
SHAPE = (2, 2, 2, 2, 8, 4)
IMG_ORDER = ("y", "zh", "zl", "xh", "xl", "c")
TXT_ORDER = ("zl", "xh", "xl", "c", "y", "zh")
PEERS = 16
CHUNKS = 4
MIB = 1 << 20


def device_index(x, y, z, c):
    return ((((z % 2) * 4 + x) * 2 + c) * 8 + y) * 4 + z // 2


def exchange_groups():
    text = [
        [device_index(x, y, z, 0) for x in (first, first + 1) for y in range(8)]
        for first in (0, 2)
        for z in range(8)
    ]
    image = [
        [device_index(x, y, z, 1) for x in (first, 3 - first) for z in range(8)]
        for first in (0, 1)
        for y in range(8)
    ]
    return text + image


def exchange(blocks):
    return lax.all_to_all(blocks, NAMES, 0, 0, axis_index_groups=exchange_groups(), tiled=False)


def swap_cores(block):
    return lax.ppermute(block, "c", [(0, 1), (1, 0)])


def unit_rows(embedded):
    values = embedded.astype(jnp.float32)
    inverse = lax.rsqrt(jnp.sum(values * values, axis=1, keepdims=True) + EPS)
    return (values * inverse, inverse)


def project_back(grad, unit, inverse):
    inner = jnp.sum(unit * grad, axis=1, keepdims=True)
    return (grad - unit * inner) * inverse


def spread_kernel(image, text, received, copies):
    speaks_text = lax.axis_index("c") == 0
    own = jnp.where(speaks_text, text[...].astype(jnp.float32), image[...].astype(jnp.float32))
    rows = own.shape[0]
    own = unit_rows(own)[0].astype(jnp.bfloat16)
    other = unit_rows(received[...])[0].astype(jnp.bfloat16)
    for peer in range(PEERS):
        copies[peer, :rows, :] = own
        copies[peer, rows:, :] = other


def global_rows(index, is_text, rows):
    x = lax.axis_index("xh") * 2 + lax.axis_index("xl")
    row = index % rows
    slot = (index // rows) % 2
    peer = index // (2 * rows)
    side, ring = peer // 8, peer % 8
    text = (
        ((lax.axis_index("zl") * 4 + lax.axis_index("xh") * 2 + side) * 2 + slot) * 8 + ring
    ) * 4 + lax.axis_index("zh")
    low = jnp.minimum(x, 3 - x)
    across = low + side * (3 - 2 * low)
    image = ((lax.axis_index("y") * 8 + ring) * 4 + across) * 2 + 1 - slot
    return jnp.where(is_text, text, image) * rows + row


def tile_kernel(rows, scalars, mine, theirs, grad):
    speaks_text = lax.axis_index("c") == 0
    scale, bias = scalars[0], scalars[1]
    total = mine.shape[0]
    part = total // CHUNKS
    there = theirs[...]
    there_ids = global_rows(
        lax.broadcasted_iota(jnp.int32, (1, total), 1), jnp.logical_not(speaks_text), rows
    )
    for start in range(0, total, part):
        here = mine[start : start + part, :]
        scores = lax.dot_general(here, there, (((1,), (1,)), ((), ())), preferred_element_type=jnp.float32)
        here_ids = global_rows(start + lax.broadcasted_iota(jnp.int32, (part, 1), 0), speaks_text, rows)
        match = jnp.where(here_ids == there_ids, 1.0, 0.0)
        weights = (jax.nn.sigmoid(scale * scores + bias) - match).astype(jnp.bfloat16)
        grad[start : start + part, :] = jnp.dot(
            weights, there, preferred_element_type=jnp.float32
        ).astype(jnp.bfloat16)


def sum_kernel(parts, own, other):
    rows = own.shape[0]
    own[...] = jnp.sum(parts[:, :rows, :].astype(jnp.float32), axis=0)
    other[...] = jnp.sum(parts[:, rows:, :].astype(jnp.float32), axis=0)


def finish_kernel(scalars, summed, received, image, text, grad_image, grad_text):
    speaks_text = lax.axis_index("c") == 0
    scale = scalars[0]
    own, other = scale * summed[...], scale * received[...]
    img_unit, img_inv = unit_rows(image[...])
    txt_unit, txt_inv = unit_rows(text[...])
    grad_image[...] = project_back(jnp.where(speaks_text, other, own), img_unit, img_inv)
    grad_text[...] = project_back(jnp.where(speaks_text, own, other), txt_unit, txt_inv)


SMEM = pl.BlockSpec(memory_space=pltpu.SMEM)
VMEM = pl.BlockSpec(memory_space=pltpu.VMEM)


def per_device(image_emb, text_emb, logit_scale, logit_bias):
    rows, width = image_emb.shape
    total = PEERS * 2 * rows
    scalars = jnp.concatenate([logit_scale, logit_bias])

    received = swap_cores(jnp.where(lax.axis_index("c") == 0, image_emb, text_emb))
    copies = pl.pallas_call(
        spread_kernel,
        out_shape=jax.ShapeDtypeStruct((PEERS, 2 * rows, width), jnp.bfloat16),
        in_specs=[VMEM, VMEM, VMEM],
        out_specs=VMEM,
        name="spread",
    )(image_emb, text_emb, received)
    mine = exchange(copies).reshape(total, width)
    theirs = swap_cores(mine)

    grad = pl.pallas_call(
        lambda *refs: tile_kernel(rows, *refs),
        out_shape=jax.ShapeDtypeStruct((total, width), jnp.bfloat16),
        in_specs=[SMEM, VMEM, VMEM],
        out_specs=VMEM,
        compiler_params=pltpu.CompilerParams(vmem_limit_bytes=40 * MIB),
        cost_estimate=pl.CostEstimate(
            flops=4 * total * total * width, bytes_accessed=6 * total * width, transcendentals=total * total
        ),
        name="tile",
    )(scalars, mine, theirs)

    parts = exchange(grad.reshape(PEERS, 2 * rows, width))
    out = jax.ShapeDtypeStruct((rows, width), jnp.float32)
    own, other = pl.pallas_call(
        sum_kernel,
        out_shape=(out, out),
        in_specs=[VMEM],
        out_specs=(VMEM, VMEM),
        name="sum",
    )(parts)
    return pl.pallas_call(
        finish_kernel,
        out_shape=(out, out),
        in_specs=[SMEM, VMEM, VMEM, VMEM, VMEM],
        out_specs=(VMEM, VMEM),
        name="finish",
    )(scalars, own, swap_cores(other), image_emb, text_emb)


def solution(mesh):
    fine = Mesh(mesh.devices.reshape(SHAPE), NAMES)
    return jax.shard_map(
        per_device,
        mesh=fine,
        in_specs=(P(IMG_ORDER, None), P(TXT_ORDER, None), P(), P()),
        out_specs=(P(IMG_ORDER, None), P(TXT_ORDER, None)),
        check_vma=False,
    )
```

```python
import jax
import jax.numpy as jnp
from jax import lax
from jax.experimental import pallas as pl
from jax.experimental.pallas import tpu as pltpu
from jax.sharding import Mesh, PartitionSpec as P

EPS = 1e-06
NAMES = ("zl", "xh", "xl", "c", "y", "zh")
SHAPE = (2, 2, 2, 2, 8, 4)
IMG_ORDER = ("y", "zh", "zl", "xh", "xl", "c")
TXT_ORDER = ("zl", "xh", "xl", "c", "y", "zh")
PEERS = 16
CHUNKS = 4
MIB = 1 << 20


def device_index(x, y, z, c):
    return ((((z % 2) * 4 + x) * 2 + c) * 8 + y) * 4 + z // 2


def exchange_groups():
    text = [
        [device_index(x, y, z, 0) for x in (first, first + 1) for y in range(8)]
        for first in (0, 2)
        for z in range(8)
    ]
    image = [
        [device_index(x, y, z, 1) for x in (first, 3 - first) for z in range(8)]
        for first in (0, 1)
        for y in range(8)
    ]
    return text + image


def exchange(blocks):
    return lax.all_to_all(blocks, NAMES, 0, 0, axis_index_groups=exchange_groups(), tiled=False)


def swap_cores(block):
    return lax.ppermute(block, "c", [(0, 1), (1, 0)])


def unit_rows(embedded):
    values = embedded.astype(jnp.float32)
    inverse = lax.rsqrt(jnp.sum(values * values, axis=1, keepdims=True) + EPS)
    return (values * inverse, inverse)


def project_back(grad, unit, inverse):
    inner = jnp.sum(unit * grad, axis=1, keepdims=True)
    return (grad - unit * inner) * inverse


def spread_kernel(image, text, received, copies):
    speaks_text = lax.axis_index("c") == 0
    own = jnp.where(speaks_text, text[...].astype(jnp.float32), image[...].astype(jnp.float32))
    rows = own.shape[0]
    own = unit_rows(own)[0].astype(jnp.bfloat16)
    other = unit_rows(received[...])[0].astype(jnp.bfloat16)
    for peer in range(PEERS):
        copies[peer, :rows, :] = own
        copies[peer, rows:, :] = other


def global_rows(index, is_text, rows):
    x = lax.axis_index("xh") * 2 + lax.axis_index("xl")
    row = index % rows
    slot = (index // rows) % 2
    peer = index // (2 * rows)
    side, ring = peer // 8, peer % 8
    text = (
        ((lax.axis_index("zl") * 4 + lax.axis_index("xh") * 2 + side) * 2 + slot) * 8 + ring
    ) * 4 + lax.axis_index("zh")
    low = jnp.minimum(x, 3 - x)
    across = low + side * (3 - 2 * low)
    image = ((lax.axis_index("y") * 8 + ring) * 4 + across) * 2 + 1 - slot
    return jnp.where(is_text, text, image) * rows + row


def tile_kernel(rows, scalars, mine, theirs, grad):
    speaks_text = lax.axis_index("c") == 0
    scale, bias = scalars[0], scalars[1]
    total = mine.shape[0]
    part = total // CHUNKS
    there = theirs[...]
    there_ids = global_rows(
        lax.broadcasted_iota(jnp.int32, (1, total), 1), jnp.logical_not(speaks_text), rows
    )
    for start in range(0, total, part):
        here = mine[start : start + part, :]
        scores = lax.dot_general(here, there, (((1,), (1,)), ((), ())), preferred_element_type=jnp.float32)
        here_ids = global_rows(start + lax.broadcasted_iota(jnp.int32, (part, 1), 0), speaks_text, rows)
        match = jnp.where(here_ids == there_ids, 1.0, 0.0)
        weights = (jax.nn.sigmoid(scale * scores + bias) - match).astype(jnp.bfloat16)
        grad[start : start + part, :] = jnp.dot(
            weights, there, preferred_element_type=jnp.float32
        ).astype(jnp.bfloat16)


def sum_kernel(parts, own, other):
    rows = own.shape[0]
    own[...] = jnp.sum(parts[:, :rows, :].astype(jnp.float32), axis=0)
    other[...] = jnp.sum(parts[:, rows:, :].astype(jnp.float32), axis=0)


def finish_kernel(scalars, summed, received, image, text, grad_image, grad_text):
    speaks_text = lax.axis_index("c") == 0
    scale = scalars[0]
    own, other = scale * summed[...], scale * received[...]
    img_unit, img_inv = unit_rows(image[...])
    txt_unit, txt_inv = unit_rows(text[...])
    grad_image[...] = project_back(jnp.where(speaks_text, other, own), img_unit, img_inv)
    grad_text[...] = project_back(jnp.where(speaks_text, own, other), txt_unit, txt_inv)


SMEM = pl.BlockSpec(memory_space=pltpu.SMEM)
VMEM = pl.BlockSpec(memory_space=pltpu.VMEM)
SMALL = pltpu.CompilerParams(vmem_limit_bytes=8 * MIB)


def per_device(image_emb, text_emb, logit_scale, logit_bias):
    rows, width = image_emb.shape
    total = PEERS * 2 * rows
    scalars = jnp.concatenate([logit_scale, logit_bias])

    received = swap_cores(jnp.where(lax.axis_index("c") == 0, image_emb, text_emb))
    copies = pl.pallas_call(
        spread_kernel,
        out_shape=jax.ShapeDtypeStruct((PEERS, 2 * rows, width), jnp.bfloat16),
        in_specs=[VMEM, VMEM, VMEM],
        out_specs=VMEM,
        compiler_params=SMALL,
        name="spread",
    )(image_emb, text_emb, received)
    mine = exchange(copies).reshape(total, width)
    theirs = swap_cores(mine)

    grad = pl.pallas_call(
        lambda *refs: tile_kernel(rows, *refs),
        out_shape=jax.ShapeDtypeStruct((total, width), jnp.bfloat16),
        in_specs=[SMEM, VMEM, VMEM],
        out_specs=VMEM,
        compiler_params=pltpu.CompilerParams(vmem_limit_bytes=40 * MIB),
        cost_estimate=pl.CostEstimate(
            flops=4 * total * total * width, bytes_accessed=6 * total * width, transcendentals=total * total
        ),
        name="tile",
    )(scalars, mine, theirs)

    parts = exchange(grad.reshape(PEERS, 2 * rows, width))
    out = jax.ShapeDtypeStruct((rows, width), jnp.float32)
    own, other = pl.pallas_call(
        sum_kernel,
        out_shape=(out, out),
        in_specs=[VMEM],
        out_specs=(VMEM, VMEM),
        compiler_params=SMALL,
        name="sum",
    )(parts)
    return pl.pallas_call(
        finish_kernel,
        out_shape=(out, out),
        in_specs=[SMEM, VMEM, VMEM, VMEM, VMEM],
        out_specs=(VMEM, VMEM),
        compiler_params=SMALL,
        name="finish",
    )(scalars, own, swap_cores(other), image_emb, text_emb)


def solution(mesh):
    fine = Mesh(mesh.devices.reshape(SHAPE), NAMES)
    return jax.shard_map(
        per_device,
        mesh=fine,
        in_specs=(P(IMG_ORDER, None), P(TXT_ORDER, None), P(), P()),
        out_specs=(P(IMG_ORDER, None), P(TXT_ORDER, None)),
        check_vma=False,
    )
```

```python
import jax
import jax.numpy as jnp
from jax import lax
from jax.experimental import pallas as pl
from jax.experimental.pallas import tpu as pltpu
from jax.sharding import Mesh, PartitionSpec as P

EPS = 1e-06
NAMES = ("zl", "xh", "xl", "c", "y", "zh")
SHAPE = (2, 2, 2, 2, 8, 4)
IMG_ORDER = ("y", "zh", "zl", "xh", "xl", "c")
TXT_ORDER = ("zl", "xh", "xl", "c", "y", "zh")
RING = 8
COLORS = 4
MIB = 1 << 20


def device_index(x, y, z, c):
    return ((((z % 2) * 4 + x) * 2 + c) * 8 + y) * 4 + z // 2


def speaker(kind, line, pair, ring, side):
    if kind == 0:
        return device_index(2 * pair + side, ring % RING, line, 0)
    return device_index(3 - pair if side else pair, line, ring % RING, 1)


def lines():
    return [(kind, line, pair) for kind in (0, 1) for line in range(RING) for pair in (0, 1)]


def color_groups():
    return [
        [speaker(*line, color + ring, side) for ring, side in ((0, 0), (4, 0), (2, 1), (6, 1))]
        for line in lines()
        for color in range(COLORS)
    ]


def links(step, flip):
    return [
        (speaker(*line, ring + step, side ^ flip), speaker(*line, ring, side))
        for line in lines()
        for ring in range(RING)
        for side in (0, 1)
    ]


NEIGHBOURS = ((1, 0), (-1, 0), (0, 1))


def exchange(blocks):
    return lax.all_to_all(blocks, NAMES, 0, 0, axis_index_groups=color_groups(), tiled=False)


def take(block, neighbour):
    return lax.ppermute(block, NAMES, links(*neighbour))


def give(block, neighbour):
    return lax.ppermute(block, NAMES, [(here, there) for there, here in links(*neighbour)])


def swap_cores(block):
    return lax.ppermute(block, "c", [(0, 1), (1, 0)])


def unit_rows(embedded):
    values = embedded.astype(jnp.float32)
    inverse = lax.rsqrt(jnp.sum(values * values, axis=1, keepdims=True) + EPS)
    return (values * inverse, inverse)


def project_back(grad, unit, inverse):
    inner = jnp.sum(unit * grad, axis=1, keepdims=True)
    return (grad - unit * inner) * inverse


def spread_kernel(own, received, copies):
    rows = own.shape[0]
    first = unit_rows(own[...])[0].astype(jnp.bfloat16)
    second = unit_rows(received[...])[0].astype(jnp.bfloat16)
    for peer in range(COLORS):
        copies[peer, :rows, :] = first
        copies[peer, rows:, :] = second


def global_rows(index, is_text, rows):
    x = lax.axis_index("xh") * 2 + lax.axis_index("xl")
    z = lax.axis_index("zh") * 2 + lax.axis_index("zl")
    row = index % rows
    slot = (index // rows) % 2
    member = (index // (2 * rows)) % COLORS
    chunk = index // (2 * rows * COLORS)
    side = member // 2
    shift = chunk ^ (chunk // 2)
    place = jnp.where(
        is_text, lax.axis_index("y") + 2 * lax.axis_index("xl"), z + 2 * lax.axis_index("xh")
    )
    ring = ((place + shift) % COLORS + 4 * (member % 2) + 2 * side) % RING
    text = (
        ((lax.axis_index("zl") * 4 + lax.axis_index("xh") * 2 + side) * 2 + slot) * 8 + ring
    ) * 4 + lax.axis_index("zh")
    low = jnp.minimum(x, 3 - x)
    across = low + side * (3 - 2 * low)
    image = ((lax.axis_index("y") * 8 + ring) * 4 + across) * 2 + 1 - slot
    return jnp.where(is_text, text, image) * rows + row


def tile_kernel(rows, chunk, scalars, mine, theirs, grad):
    speaks_text = lax.axis_index("c") == 0
    scale, bias = scalars[0], scalars[1]
    part, total = mine.shape[0], theirs.shape[0]
    there = theirs[...]
    there_ids = global_rows(
        lax.broadcasted_iota(jnp.int32, (1, total), 1), jnp.logical_not(speaks_text), rows
    )
    here_ids = global_rows(chunk * part + lax.broadcasted_iota(jnp.int32, (part, 1), 0), speaks_text, rows)
    scores = lax.dot_general(mine[...], there, (((1,), (1,)), ((), ())), preferred_element_type=jnp.float32)
    match = jnp.where(here_ids == there_ids, 1.0, 0.0)
    weights = (jax.nn.sigmoid(scale * scores + bias) - match).astype(jnp.bfloat16)
    grad[...] = jnp.dot(weights, there, preferred_element_type=jnp.float32).astype(grad.dtype)


def sum_kernel(parts, own, other):
    rows = own.shape[0]
    own[...] = jnp.sum(parts[:, :rows, :].astype(jnp.float32), axis=0)
    other[...] = jnp.sum(parts[:, rows:, :].astype(jnp.float32), axis=0)


def finish_kernel(scalars, summed, received, image, text, grad_image, grad_text):
    speaks_text = lax.axis_index("c") == 0
    scale = scalars[0]
    own, other = scale * summed[...], scale * received[...]
    img_unit, img_inv = unit_rows(image[...])
    txt_unit, txt_inv = unit_rows(text[...])
    grad_image[...] = project_back(jnp.where(speaks_text, other, own), img_unit, img_inv)
    grad_text[...] = project_back(jnp.where(speaks_text, own, other), txt_unit, txt_inv)


SMEM = pl.BlockSpec(memory_space=pltpu.SMEM)
VMEM = pl.BlockSpec(memory_space=pltpu.VMEM)
SMALL = pltpu.CompilerParams(vmem_limit_bytes=8 * MIB)
LARGE = pltpu.CompilerParams(vmem_limit_bytes=24 * MIB)


def per_device(image_emb, text_emb, logit_scale, logit_bias):
    rows, width = image_emb.shape
    part = COLORS * 2 * rows
    total = COLORS * part
    scalars = jnp.concatenate([logit_scale, logit_bias])

    speaks_text = lax.axis_index("c") == 0
    kept = jnp.where(speaks_text, text_emb, image_emb)
    received = swap_cores(jnp.where(speaks_text, image_emb, text_emb))
    copies = pl.pallas_call(
        spread_kernel,
        out_shape=jax.ShapeDtypeStruct((COLORS, 2 * rows, width), jnp.bfloat16),
        in_specs=[VMEM, VMEM],
        out_specs=VMEM,
        compiler_params=SMALL,
        name="spread",
    )(kept, received)
    own = exchange(copies).reshape(part, width)
    mine = [own] + [take(own, neighbour) for neighbour in NEIGHBOURS]
    theirs = jnp.concatenate([swap_cores(chunk) for chunk in mine], axis=0)

    def tile(chunk, dtype):
        return pl.pallas_call(
            lambda *refs: tile_kernel(rows, chunk, *refs),
            out_shape=jax.ShapeDtypeStruct((part, width), dtype),
            in_specs=[SMEM, VMEM, VMEM],
            out_specs=VMEM,
            compiler_params=LARGE,
            cost_estimate=pl.CostEstimate(
                flops=4 * part * total * width,
                bytes_accessed=2 * (total + 2 * part) * width,
                transcendentals=part * total,
            ),
            name="tile",
        )(scalars, mine[chunk], theirs)

    partial = [give(tile(1 + k, jnp.bfloat16), neighbour) for k, neighbour in enumerate(NEIGHBOURS)]
    summed = tile(0, jnp.float32)
    for block in partial:
        summed = summed + block.astype(jnp.float32)
    parts = exchange(summed.astype(jnp.bfloat16).reshape(COLORS, 2 * rows, width))
    out = jax.ShapeDtypeStruct((rows, width), jnp.float32)
    own, other = pl.pallas_call(
        sum_kernel,
        out_shape=(out, out),
        in_specs=[VMEM],
        out_specs=(VMEM, VMEM),
        compiler_params=SMALL,
        name="sum",
    )(parts)
    return pl.pallas_call(
        finish_kernel,
        out_shape=(out, out),
        in_specs=[SMEM, VMEM, VMEM, VMEM, VMEM],
        out_specs=(VMEM, VMEM),
        compiler_params=SMALL,
        name="finish",
    )(scalars, own, swap_cores(other), image_emb, text_emb)


def solution(mesh):
    fine = Mesh(mesh.devices.reshape(SHAPE), NAMES)
    return jax.shard_map(
        per_device,
        mesh=fine,
        in_specs=(P(IMG_ORDER, None), P(TXT_ORDER, None), P(), P()),
        out_specs=(P(IMG_ORDER, None), P(TXT_ORDER, None)),
        check_vma=False,
    )
```

```python
import jax
import jax.numpy as jnp
from jax import lax
from jax.experimental import pallas as pl
from jax.experimental.pallas import tpu as pltpu
from jax.sharding import Mesh, PartitionSpec as P

EPS = 1e-06
NAMES = ("zl", "xh", "xl", "c", "y", "zh")
SHAPE = (2, 2, 2, 2, 8, 4)
IMG_ORDER = ("y", "zh", "zl", "xh", "xl", "c")
TXT_ORDER = ("zl", "xh", "xl", "c", "y", "zh")
RING = 8
COLORS = 4
MIB = 1 << 20


def device_index(x, y, z, c):
    return ((((z % 2) * 4 + x) * 2 + c) * 8 + y) * 4 + z // 2


def speaker(kind, line, pair, ring, side):
    if kind == 0:
        return device_index(2 * pair + side, ring % RING, line, 0)
    return device_index(3 - pair if side else pair, line, ring % RING, 1)


def lines():
    return [(kind, line, pair) for kind in (0, 1) for line in range(RING) for pair in (0, 1)]


def color_groups():
    return [
        [speaker(*line, color + ring, side) for ring, side in ((0, 0), (4, 0), (2, 1), (6, 1))]
        for line in lines()
        for color in range(COLORS)
    ]


def links(step, flip):
    return [
        (speaker(*line, ring + step, side ^ flip), speaker(*line, ring, side))
        for line in lines()
        for ring in range(RING)
        for side in (0, 1)
    ]


NEIGHBOURS = ((1, 0), (-1, 0), (0, 1))


def exchange(blocks):
    return lax.all_to_all(blocks, NAMES, 0, 0, axis_index_groups=color_groups(), tiled=False)


def take(block, neighbour):
    return lax.ppermute(block, NAMES, links(*neighbour))


def give(block, neighbour):
    return lax.ppermute(block, NAMES, [(here, there) for there, here in links(*neighbour)])


def swap_cores(block):
    return lax.ppermute(block, "c", [(0, 1), (1, 0)])


def unit_rows(embedded):
    values = embedded.astype(jnp.float32)
    inverse = lax.rsqrt(jnp.sum(values * values, axis=1, keepdims=True) + EPS)
    return (values * inverse, inverse)


def project_back(grad, unit, inverse):
    inner = jnp.sum(unit * grad, axis=1, keepdims=True)
    return (grad - unit * inner) * inverse


def spread_kernel(own, received, copies):
    rows = own.shape[0]
    first = unit_rows(own[...])[0].astype(jnp.bfloat16)
    second = unit_rows(received[...])[0].astype(jnp.bfloat16)
    for peer in range(COLORS):
        copies[peer, :rows, :] = first
        copies[peer, rows:, :] = second


def global_rows(index, is_text, rows):
    bits = rows.bit_length() - 1
    x = lax.axis_index("xh") * 2 + lax.axis_index("xl")
    z = lax.axis_index("zh") * 2 + lax.axis_index("zl")
    low = jnp.minimum(x, 3 - x)
    text = ((lax.axis_index("zl") * 4 + lax.axis_index("xh") * 2) * 2 * 8) * 4 + lax.axis_index("zh")
    image = (lax.axis_index("y") * 8 * 4 + low) * 2 + 1
    place = jnp.where(
        is_text, lax.axis_index("y") + 2 * lax.axis_index("xl"), z + 2 * lax.axis_index("xh")
    )
    first = jnp.where(is_text, text, image) * rows
    per_side = jnp.where(is_text, 64, 2 * (3 - 2 * low)) * rows
    per_slot = jnp.where(is_text, 32, -1) * rows
    per_ring = jnp.where(is_text, 4, 8) * rows

    member = (index >> (bits + 1)) & (COLORS - 1)
    chunk = index >> (bits + 3)
    side = member >> 1
    color = (place + (chunk ^ (chunk >> 1))) & (COLORS - 1)
    ring = (color + ((member & 1) << 2) + (side << 1)) & (RING - 1)
    slot = (index >> bits) & 1
    return first + per_side * side + per_slot * slot + per_ring * ring + (index & (rows - 1))


LOG2_E = 1.4426950408889634


def tile_kernel(rows, chunks, scalars, *refs):
    mine, theirs, grads = refs[: len(chunks)], refs[len(chunks)], refs[len(chunks) + 1 :]
    speaks_text = lax.axis_index("c") == 0
    slope, offset = -LOG2_E * scalars[0:1, 0:1], -LOG2_E * scalars[0:1, 1:2]
    part, total = mine[0].shape[0], theirs.shape[0]
    there_ids = global_rows(
        lax.broadcasted_iota(jnp.int32, (1, total), 1), jnp.logical_not(speaks_text), rows
    )

    def weigh(k):
        scores = lax.dot_general(
            mine[k][...], theirs[...], (((1,), (1,)), ((), ())), preferred_element_type=jnp.float32
        )
        here_ids = global_rows(
            chunks[k] * part + lax.broadcasted_iota(jnp.int32, (part, 1), 0), speaks_text, rows
        )
        match = jnp.where(here_ids == there_ids, 1.0, 0.0)
        return (1.0 / (1.0 + jnp.exp2(scores * slope + offset)) - match).astype(jnp.bfloat16)

    def finish(k, weights):
        grads[k][...] = jnp.dot(weights, theirs[...], preferred_element_type=jnp.float32).astype(
            grads[k].dtype
        )

    before = None
    for k in range(len(chunks)):
        weights = weigh(k)
        if k > 0:
            finish(k - 1, before)
        before = weights
    finish(len(chunks) - 1, before)


def sum_kernel(parts, own, other):
    rows = own.shape[0]
    own[...] = jnp.sum(parts[:, :rows, :].astype(jnp.float32), axis=0)
    other[...] = jnp.sum(parts[:, rows:, :].astype(jnp.float32), axis=0)


def finish_kernel(scalars, summed, received, image, text, grad_image, grad_text):
    speaks_text = lax.axis_index("c") == 0
    scale = scalars[0:1, 0:1]
    own, other = scale * summed[...], scale * received[...]
    img_unit, img_inv = unit_rows(image[...])
    txt_unit, txt_inv = unit_rows(text[...])
    grad_image[...] = project_back(jnp.where(speaks_text, other, own), img_unit, img_inv)
    grad_text[...] = project_back(jnp.where(speaks_text, own, other), txt_unit, txt_inv)


VMEM = pl.BlockSpec(memory_space=pltpu.VMEM)
SMALL = pltpu.CompilerParams(vmem_limit_bytes=8 * MIB)
LARGE = pltpu.CompilerParams(vmem_limit_bytes=24 * MIB)


def per_device(image_emb, text_emb, logit_scale, logit_bias):
    rows, width = image_emb.shape
    part = COLORS * 2 * rows
    total = COLORS * part
    scalars = jnp.concatenate([logit_scale, logit_bias]).reshape(1, 2)

    speaks_text = lax.axis_index("c") == 0
    kept = jnp.where(speaks_text, text_emb, image_emb)
    received = swap_cores(jnp.where(speaks_text, image_emb, text_emb))
    copies = pl.pallas_call(
        spread_kernel,
        out_shape=jax.ShapeDtypeStruct((COLORS, 2 * rows, width), jnp.bfloat16),
        in_specs=[VMEM, VMEM],
        out_specs=VMEM,
        compiler_params=SMALL,
        name="spread",
    )(kept, received)
    own = exchange(copies).reshape(part, width)
    mine = [own] + [take(own, neighbour) for neighbour in NEIGHBOURS]
    theirs = [swap_cores(chunk) for chunk in mine]
    theirs = jnp.concatenate(theirs, axis=0)

    def tile(chunks, dtype):
        count = len(chunks)
        return pl.pallas_call(
            lambda *refs: tile_kernel(rows, chunks, *refs),
            out_shape=[jax.ShapeDtypeStruct((part, width), dtype)] * count,
            in_specs=[VMEM] * (count + 2),
            out_specs=[VMEM] * count,
            compiler_params=LARGE,
            cost_estimate=pl.CostEstimate(
                flops=4 * count * part * total * width,
                bytes_accessed=2 * (total + 2 * count * part) * width,
                transcendentals=count * part * total,
            ),
            name="tile",
        )(scalars, *[mine[chunk] for chunk in chunks], theirs)

    partial = [
        give(block, neighbour) for block, neighbour in zip(tile((1, 2, 3), jnp.bfloat16), NEIGHBOURS)
    ]
    (summed,) = tile((0,), jnp.float32)
    for block in partial:
        summed = summed + block.astype(jnp.float32)
    parts = exchange(summed.astype(jnp.bfloat16).reshape(COLORS, 2 * rows, width))
    out = jax.ShapeDtypeStruct((rows, width), jnp.float32)
    own, other = pl.pallas_call(
        sum_kernel,
        out_shape=(out, out),
        in_specs=[VMEM],
        out_specs=(VMEM, VMEM),
        compiler_params=SMALL,
        name="sum",
    )(parts)
    return pl.pallas_call(
        finish_kernel,
        out_shape=(out, out),
        in_specs=[VMEM] * 5,
        out_specs=(VMEM, VMEM),
        compiler_params=SMALL,
        name="finish",
    )(scalars, own, swap_cores(other), image_emb, text_emb)


def solution(mesh):
    fine = Mesh(mesh.devices.reshape(SHAPE), NAMES)
    return jax.shard_map(
        per_device,
        mesh=fine,
        in_specs=(P(IMG_ORDER, None), P(TXT_ORDER, None), P(), P()),
        out_specs=(P(IMG_ORDER, None), P(TXT_ORDER, None)),
        check_vma=False,
    )
```

```python
import jax
import jax.numpy as jnp
from jax import lax
from jax.experimental import pallas as pl
from jax.experimental.pallas import tpu as pltpu
from jax.sharding import Mesh, PartitionSpec as P

EPS = 1e-06
NAMES = ("zl", "xh", "xl", "c", "y", "zh")
SHAPE = (2, 2, 2, 2, 8, 4)
IMG_ORDER = ("y", "zh", "zl", "xh", "xl", "c")
TXT_ORDER = ("zl", "xh", "xl", "c", "y", "zh")
RING = 8
COLORS = 4
MIB = 1 << 20


def device_index(x, y, z, c):
    return ((((z % 2) * 4 + x) * 2 + c) * 8 + y) * 4 + z // 2


def speaker(kind, line, pair, ring, side):
    if kind == 0:
        return device_index(2 * pair + side, ring % RING, line, 0)
    return device_index(3 - pair if side else pair, line, ring % RING, 1)


def lines():
    return [(kind, line, pair) for kind in (0, 1) for line in range(RING) for pair in (0, 1)]


def color_groups():
    return [
        [speaker(*line, color + ring, side) for ring, side in ((0, 0), (4, 0), (2, 1), (6, 1))]
        for line in lines()
        for color in range(COLORS)
    ]


def links(step, flip):
    return [
        (speaker(*line, ring + step, side ^ flip), speaker(*line, ring, side))
        for line in lines()
        for ring in range(RING)
        for side in (0, 1)
    ]


NEIGHBOURS = ((1, 0), (-1, 0), (0, 1))


def exchange(blocks):
    return lax.all_to_all(blocks, NAMES, 0, 0, axis_index_groups=color_groups(), tiled=False)


def take(block, neighbour):
    return lax.ppermute(block, NAMES, links(*neighbour))


def give(block, neighbour):
    return lax.ppermute(block, NAMES, [(here, there) for there, here in links(*neighbour)])


def swap_cores(block):
    return lax.ppermute(block, "c", [(0, 1), (1, 0)])


def gather_cores(block):
    return lax.all_gather(block, "c", axis=0, tiled=True)


def unit_rows(embedded):
    values = embedded.astype(jnp.float32)
    inverse = lax.rsqrt(jnp.sum(values * values, axis=1, keepdims=True) + EPS)
    return (values * inverse, inverse)


def project_back(grad, unit, inverse):
    inner = jnp.sum(unit * grad, axis=1, keepdims=True)
    return (grad - unit * inner) * inverse


def from_other_core(pair):
    rows = pair.shape[0] // 2
    return pair[pl.ds(pl.multiple_of((1 - lax.axis_index("c")) * rows, rows), rows), :]


def spread_kernel(own, pair, copies):
    rows = own.shape[0]
    first = unit_rows(own[...])[0].astype(jnp.bfloat16)
    second = unit_rows(from_other_core(pair))[0].astype(jnp.bfloat16)
    for peer in range(COLORS):
        copies[peer, :rows, :] = first
        copies[peer, rows:, :] = second


def global_rows(index, is_text, rows):
    bits = rows.bit_length() - 1
    x = lax.axis_index("xh") * 2 + lax.axis_index("xl")
    z = lax.axis_index("zh") * 2 + lax.axis_index("zl")
    low = jnp.minimum(x, 3 - x)
    text = ((lax.axis_index("zl") * 4 + lax.axis_index("xh") * 2) * 2 * 8) * 4 + lax.axis_index("zh")
    image = (lax.axis_index("y") * 8 * 4 + low) * 2 + 1
    place = jnp.where(
        is_text, lax.axis_index("y") + 2 * lax.axis_index("xl"), z + 2 * lax.axis_index("xh")
    )
    first = jnp.where(is_text, text, image) * rows
    per_side = jnp.where(is_text, 64, 2 * (3 - 2 * low)) * rows
    per_slot = jnp.where(is_text, 32, -1) * rows
    per_ring = jnp.where(is_text, 4, 8) * rows

    member = (index >> (bits + 1)) & (COLORS - 1)
    chunk = index >> (bits + 3)
    side = member >> 1
    color = (place + (chunk ^ (chunk >> 1))) & (COLORS - 1)
    ring = (color + ((member & 1) << 2) + (side << 1)) & (RING - 1)
    slot = (index >> bits) & 1
    return first + per_side * side + per_slot * slot + per_ring * ring + (index & (rows - 1))


LOG2_E = 1.4426950408889634


def tile_kernel(rows, chunks, scalars, *refs):
    mine, theirs, grads = refs[: len(chunks)], refs[len(chunks)], refs[len(chunks) + 1 :]
    speaks_text = lax.axis_index("c") == 0
    slope, offset = -LOG2_E * scalars[0:1, 0:1], -LOG2_E * scalars[0:1, 1:2]
    part, total = mine[0].shape[0], theirs.shape[0]
    there_ids = global_rows(
        lax.broadcasted_iota(jnp.int32, (1, total), 1), jnp.logical_not(speaks_text), rows
    )

    def weigh(k):
        scores = lax.dot_general(
            mine[k][...], theirs[...], (((1,), (1,)), ((), ())), preferred_element_type=jnp.float32
        )
        here_ids = global_rows(
            chunks[k] * part + lax.broadcasted_iota(jnp.int32, (part, 1), 0), speaks_text, rows
        )
        match = jnp.where(here_ids == there_ids, 1.0, 0.0)
        return (1.0 / (1.0 + jnp.exp2(scores * slope + offset)) - match).astype(jnp.bfloat16)

    def finish(k, weights):
        grads[k][...] = jnp.dot(weights, theirs[...], preferred_element_type=jnp.float32).astype(
            grads[k].dtype
        )

    before = None
    for k in range(len(chunks)):
        weights = weigh(k)
        if k > 0:
            finish(k - 1, before)
        before = weights
    finish(len(chunks) - 1, before)


def sum_kernel(parts, own, other):
    rows = own.shape[0]
    own[...] = jnp.sum(parts[:, :rows, :].astype(jnp.float32), axis=0)
    other[...] = jnp.sum(parts[:, rows:, :].astype(jnp.float32), axis=0)


def finish_kernel(scalars, summed, pair, image, text, grad_image, grad_text):
    speaks_text = lax.axis_index("c") == 0
    scale = scalars[0:1, 0:1]
    own, other = scale * summed[...], scale * from_other_core(pair)
    img_unit, img_inv = unit_rows(image[...])
    txt_unit, txt_inv = unit_rows(text[...])
    grad_image[...] = project_back(jnp.where(speaks_text, other, own), img_unit, img_inv)
    grad_text[...] = project_back(jnp.where(speaks_text, own, other), txt_unit, txt_inv)


VMEM = pl.BlockSpec(memory_space=pltpu.VMEM)
SMALL = pltpu.CompilerParams(vmem_limit_bytes=8 * MIB)
LARGE = pltpu.CompilerParams(vmem_limit_bytes=24 * MIB)


def per_device(image_emb, text_emb, logit_scale, logit_bias):
    rows, width = image_emb.shape
    part = COLORS * 2 * rows
    total = COLORS * part
    scalars = jnp.concatenate([logit_scale, logit_bias]).reshape(1, 2)

    speaks_text = lax.axis_index("c") == 0
    kept = jnp.where(speaks_text, text_emb, image_emb)
    pair = gather_cores(jnp.where(speaks_text, image_emb, text_emb))
    copies = pl.pallas_call(
        spread_kernel,
        out_shape=jax.ShapeDtypeStruct((COLORS, 2 * rows, width), jnp.bfloat16),
        in_specs=[VMEM, VMEM],
        out_specs=VMEM,
        compiler_params=SMALL,
        name="spread",
    )(kept, pair)
    own = exchange(copies).reshape(part, width)
    mine = [own] + [take(own, neighbour) for neighbour in NEIGHBOURS]
    theirs = [swap_cores(chunk) for chunk in mine]
    theirs = jnp.concatenate(theirs, axis=0)

    def tile(chunks, dtype):
        count = len(chunks)
        return pl.pallas_call(
            lambda *refs: tile_kernel(rows, chunks, *refs),
            out_shape=[jax.ShapeDtypeStruct((part, width), dtype)] * count,
            in_specs=[VMEM] * (count + 2),
            out_specs=[VMEM] * count,
            compiler_params=LARGE,
            cost_estimate=pl.CostEstimate(
                flops=4 * count * part * total * width,
                bytes_accessed=2 * (total + 2 * count * part) * width,
                transcendentals=count * part * total,
            ),
            name="tile",
        )(scalars, *[mine[chunk] for chunk in chunks], theirs)

    partial = [
        give(block, neighbour) for block, neighbour in zip(tile((1, 2, 3), jnp.bfloat16), NEIGHBOURS)
    ]
    (summed,) = tile((0,), jnp.float32)
    for block in partial:
        summed = summed + block.astype(jnp.float32)
    parts = exchange(summed.astype(jnp.bfloat16).reshape(COLORS, 2 * rows, width))
    out = jax.ShapeDtypeStruct((rows, width), jnp.float32)
    own, other = pl.pallas_call(
        sum_kernel,
        out_shape=(out, out),
        in_specs=[VMEM],
        out_specs=(VMEM, VMEM),
        compiler_params=SMALL,
        name="sum",
    )(parts)
    return pl.pallas_call(
        finish_kernel,
        out_shape=(out, out),
        in_specs=[VMEM] * 5,
        out_specs=(VMEM, VMEM),
        compiler_params=SMALL,
        name="finish",
    )(scalars, own, gather_cores(other), image_emb, text_emb)


def solution(mesh):
    fine = Mesh(mesh.devices.reshape(SHAPE), NAMES)
    return jax.shard_map(
        per_device,
        mesh=fine,
        in_specs=(P(IMG_ORDER, None), P(TXT_ORDER, None), P(), P()),
        out_specs=(P(IMG_ORDER, None), P(TXT_ORDER, None)),
        check_vma=False,
    )
```

```python
import jax
import jax.numpy as jnp
from jax import lax
from jax.experimental import pallas as pl
from jax.experimental.pallas import tpu as pltpu
from jax.sharding import Mesh, PartitionSpec as P

EPS = 1e-06
NAMES = ("zl", "xh", "xl", "c", "y", "zh")
SHAPE = (2, 2, 2, 2, 8, 4)
IMG_ORDER = ("y", "zh", "zl", "xh", "xl", "c")
TXT_ORDER = ("zl", "xh", "xl", "c", "y", "zh")
RING = 8
COLORS = 4
MIB = 1 << 20


def device_index(x, y, z, c):
    return ((((z % 2) * 4 + x) * 2 + c) * 8 + y) * 4 + z // 2


def speaker(kind, line, pair, ring, side):
    if kind == 0:
        return device_index(2 * pair + side, ring % RING, line, 0)
    return device_index(3 - pair if side else pair, line, ring % RING, 1)


def lines():
    return [(kind, line, pair) for kind in (0, 1) for line in range(RING) for pair in (0, 1)]


def color_groups():
    return [
        [speaker(*line, color + ring, side) for ring, side in ((0, 0), (4, 0), (2, 1), (6, 1))]
        for line in lines()
        for color in range(COLORS)
    ]


NEIGHBOURS = (
    lambda ring, side: (ring ^ 1, side),
    lambda ring, side: (((ring + 1) ^ 1) - 1, side),
    lambda ring, side: (ring, 1 - side),
)


def swap_with(block, neighbour):
    pairs = [
        (speaker(*line, *neighbour(ring, side)), speaker(*line, ring, side))
        for line in lines()
        for ring in range(RING)
        for side in (0, 1)
    ]
    return lax.ppermute(block, NAMES, pairs)


def exchange(blocks):
    return lax.all_to_all(blocks, NAMES, 0, 0, axis_index_groups=color_groups(), tiled=False)


def swap_cores(block):
    return lax.ppermute(block, "c", [(0, 1), (1, 0)])


def gather_cores(block):
    return lax.all_gather(block, "c", axis=0, tiled=True)


def unit_rows(embedded):
    values = embedded.astype(jnp.float32)
    inverse = lax.rsqrt(jnp.sum(values * values, axis=1, keepdims=True) + EPS)
    return (values * inverse, inverse)


def project_back(grad, unit, inverse):
    inner = jnp.sum(unit * grad, axis=1, keepdims=True)
    return (grad - unit * inner) * inverse


def from_other_core(pair):
    rows = pair.shape[0] // 2
    return pair[pl.ds(pl.multiple_of((1 - lax.axis_index("c")) * rows, rows), rows), :]


def spread_kernel(own, pair, copies):
    rows = own.shape[0]
    first = unit_rows(own[...])[0].astype(jnp.bfloat16)
    second = unit_rows(from_other_core(pair))[0].astype(jnp.bfloat16)
    for peer in range(COLORS):
        copies[peer, :rows, :] = first
        copies[peer, rows:, :] = second


def global_rows(index, is_text, rows):
    bits = rows.bit_length() - 1
    x = lax.axis_index("xh") * 2 + lax.axis_index("xl")
    z = lax.axis_index("zh") * 2 + lax.axis_index("zl")
    low = jnp.minimum(x, 3 - x)
    text = ((lax.axis_index("zl") * 4 + lax.axis_index("xh") * 2) * 2 * 8) * 4 + lax.axis_index("zh")
    image = (lax.axis_index("y") * 8 * 4 + low) * 2 + 1
    place = jnp.where(
        is_text, lax.axis_index("y") + 2 * lax.axis_index("xl"), z + 2 * lax.axis_index("xh")
    )
    first = jnp.where(is_text, text, image) * rows
    per_side = jnp.where(is_text, 64, 2 * (3 - 2 * low)) * rows
    per_slot = jnp.where(is_text, 32, -1) * rows
    per_ring = jnp.where(is_text, 4, 8) * rows

    member = (index >> (bits + 1)) & (COLORS - 1)
    chunk = index >> (bits + 3)
    side = member >> 1
    odd = jnp.where(is_text, lax.axis_index("y") & 1, lax.axis_index("zl"))
    step = chunk ^ (chunk >> 1)
    color = (place + step + ((odd * step) & 1) * 2) & (COLORS - 1)
    ring = (color + ((member & 1) << 2) + (side << 1)) & (RING - 1)
    slot = (index >> bits) & 1
    return first + per_side * side + per_slot * slot + per_ring * ring + (index & (rows - 1))


LOG2_E = 1.4426950408889634


def weigh(rows, scalars, mine, here_start, theirs, there_start):
    speaks_text = lax.axis_index("c") == 0
    slope, offset = -LOG2_E * scalars[0:1, 0:1], -LOG2_E * scalars[0:1, 1:2]
    scores = lax.dot_general(mine, theirs, (((1,), (1,)), ((), ())), preferred_element_type=jnp.float32)
    here_ids = global_rows(
        here_start + lax.broadcasted_iota(jnp.int32, (mine.shape[0], 1), 0), speaks_text, rows
    )
    there_ids = global_rows(
        there_start + lax.broadcasted_iota(jnp.int32, (1, theirs.shape[0]), 1),
        jnp.logical_not(speaks_text),
        rows,
    )
    match = jnp.where(here_ids == there_ids, 1.0, 0.0)
    return (1.0 / (1.0 + jnp.exp2(scores * slope + offset)) - match).astype(jnp.bfloat16)


def weigh_kernel(rows, chunks, count, scalars, *refs):
    mine, theirs, weights = refs[: len(chunks)], refs[len(chunks) : -len(chunks)], refs[-len(chunks) :]
    part = mine[0].shape[0]
    for k in range(len(chunks)):
        for j in range(count):
            weights[k][:, j * part : (j + 1) * part] = weigh(
                rows, scalars, mine[k][...], chunks[k] * part, theirs[j][...], j * part
            )


def tile_kernel(rows, chunks, early, scalars, *refs):
    count = len(chunks)
    mine, ready, theirs, grads = refs[:count], refs[count : -count - 1], refs[-count - 1], refs[-count:]
    part = mine[0].shape[0]
    done = early * part

    def weights_of(k):
        late = weigh(rows, scalars, mine[k][...], chunks[k] * part, theirs[done:, :], done)
        return jnp.concatenate([ready[k][...], late], axis=1) if early else late

    def finish(k, weights):
        grads[k][...] = jnp.dot(weights, theirs[...], preferred_element_type=jnp.float32).astype(
            grads[k].dtype
        )

    before = None
    for k in range(count):
        weights = weights_of(k)
        if k > 0:
            finish(k - 1, before)
        before = weights
    finish(count - 1, before)


def sum_kernel(parts, own, other):
    rows = own.shape[0]
    own[...] = jnp.sum(parts[:, :rows, :].astype(jnp.float32), axis=0)
    other[...] = jnp.sum(parts[:, rows:, :].astype(jnp.float32), axis=0)


def finish_kernel(scalars, summed, pair, image, text, grad_image, grad_text):
    speaks_text = lax.axis_index("c") == 0
    scale = scalars[0:1, 0:1]
    own, other = scale * summed[...], scale * from_other_core(pair)
    img_unit, img_inv = unit_rows(image[...])
    txt_unit, txt_inv = unit_rows(text[...])
    grad_image[...] = project_back(jnp.where(speaks_text, other, own), img_unit, img_inv)
    grad_text[...] = project_back(jnp.where(speaks_text, own, other), txt_unit, txt_inv)


VMEM = pl.BlockSpec(memory_space=pltpu.VMEM)
SMALL = pltpu.CompilerParams(vmem_limit_bytes=8 * MIB)
LARGE = pltpu.CompilerParams(vmem_limit_bytes=24 * MIB)


def per_device(image_emb, text_emb, logit_scale, logit_bias):
    rows, width = image_emb.shape
    part = COLORS * 2 * rows
    total = COLORS * part
    scalars = jnp.concatenate([logit_scale, logit_bias]).reshape(1, 2)

    speaks_text = lax.axis_index("c") == 0
    kept = jnp.where(speaks_text, text_emb, image_emb)
    pair = gather_cores(jnp.where(speaks_text, image_emb, text_emb))
    copies = pl.pallas_call(
        spread_kernel,
        out_shape=jax.ShapeDtypeStruct((COLORS, 2 * rows, width), jnp.bfloat16),
        in_specs=[VMEM, VMEM],
        out_specs=VMEM,
        compiler_params=SMALL,
        name="spread",
    )(kept, pair)
    own = exchange(copies).reshape(part, width)
    mine = [own] + [swap_with(own, neighbour) for neighbour in NEIGHBOURS]
    chunks = [swap_cores(chunk) for chunk in mine]
    theirs = jnp.concatenate(chunks, axis=0)
    near, early = (1, 2, 3), 3

    def call(kernel, out_shape, operands, products, name):
        return pl.pallas_call(
            kernel,
            out_shape=out_shape,
            in_specs=[VMEM] * len(operands),
            out_specs=[VMEM] * len(out_shape),
            compiler_params=LARGE,
            cost_estimate=pl.CostEstimate(
                flops=2 * products * part * part * width,
                bytes_accessed=2 * sum(operand.size for operand in operands),
                transcendentals=products * part * part // 2,
            ),
            name=name,
        )(*operands)

    def tile(rows_of, ready, dtype):
        return call(
            lambda *refs: tile_kernel(rows, rows_of, early if ready else 0, *refs),
            [jax.ShapeDtypeStruct((part, width), dtype)] * len(rows_of),
            [scalars, *[mine[chunk] for chunk in rows_of], *ready, theirs],
            len(rows_of) * (8 - (early if ready else 0)),
            "tile",
        )

    ready = call(
        lambda *refs: weigh_kernel(rows, near, early, *refs),
        [jax.ShapeDtypeStruct((part, early * part), jnp.bfloat16)] * len(near),
        [scalars, *[mine[chunk] for chunk in near], *chunks[:early]],
        len(near) * early,
        "weigh",
    )
    partial = [
        swap_with(block, neighbour) for block, neighbour in zip(tile(near, ready, jnp.bfloat16), NEIGHBOURS)
    ]
    (summed,) = tile((0,), [], jnp.float32)
    for block in partial:
        summed = summed + block.astype(jnp.float32)
    parts = exchange(summed.astype(jnp.bfloat16).reshape(COLORS, 2 * rows, width))
    out = jax.ShapeDtypeStruct((rows, width), jnp.float32)
    own, other = pl.pallas_call(
        sum_kernel,
        out_shape=(out, out),
        in_specs=[VMEM],
        out_specs=(VMEM, VMEM),
        compiler_params=SMALL,
        name="sum",
    )(parts)
    return pl.pallas_call(
        finish_kernel,
        out_shape=(out, out),
        in_specs=[VMEM] * 5,
        out_specs=(VMEM, VMEM),
        compiler_params=SMALL,
        name="finish",
    )(scalars, own, gather_cores(other), image_emb, text_emb)


def solution(mesh):
    fine = Mesh(mesh.devices.reshape(SHAPE), NAMES)
    return jax.shard_map(
        per_device,
        mesh=fine,
        in_specs=(P(IMG_ORDER, None), P(TXT_ORDER, None), P(), P()),
        out_specs=(P(IMG_ORDER, None), P(TXT_ORDER, None)),
        check_vma=False,
    )
```

```python
import jax
import jax.numpy as jnp
from jax import lax
from jax.experimental import pallas as pl
from jax.experimental.pallas import tpu as pltpu
from jax.sharding import Mesh, PartitionSpec as P

EPS = 1e-06
NAMES = ("zl", "xh", "xl", "c", "y", "zh")
SHAPE = (2, 2, 2, 2, 8, 4)
IMG_ORDER = ("y", "zh", "zl", "xh", "xl", "c")
TXT_ORDER = ("zl", "xh", "xl", "c", "y", "zh")
RING = 8
COLORS = 4
MIB = 1 << 20


def device_index(x, y, z, c):
    return ((((z % 2) * 4 + x) * 2 + c) * 8 + y) * 4 + z // 2


def speaker(kind, line, pair, ring, side):
    if kind == 0:
        return device_index(2 * pair + side, ring % RING, line, 0)
    return device_index(3 - pair if side else pair, line, ring % RING, 1)


def lines():
    return [(kind, line, pair) for kind in (0, 1) for line in range(RING) for pair in (0, 1)]


def color_groups():
    return [
        [speaker(*line, color + ring, side) for ring, side in ((0, 0), (4, 0), (2, 1), (6, 1))]
        for line in lines()
        for color in range(COLORS)
    ]


NEIGHBOURS = (
    lambda ring, side: (ring ^ 1, side),
    lambda ring, side: (((ring + 1) ^ 1) - 1, side),
    lambda ring, side: (ring, 1 - side),
)


def swap_with(block, neighbour):
    pairs = [
        (speaker(*line, *neighbour(ring, side)), speaker(*line, ring, side))
        for line in lines()
        for ring in range(RING)
        for side in (0, 1)
    ]
    return lax.ppermute(block, NAMES, pairs)


def exchange(blocks):
    return lax.all_to_all(blocks, NAMES, 0, 0, axis_index_groups=color_groups(), tiled=False)


def swap_cores(block):
    return lax.ppermute(block, "c", [(0, 1), (1, 0)])


def gather_cores(block):
    return lax.all_gather(block, "c", axis=0, tiled=True)


def unit_rows(embedded):
    values = embedded.astype(jnp.float32)
    inverse = lax.rsqrt(jnp.sum(values * values, axis=1, keepdims=True) + EPS)
    return (values * inverse, inverse)


def project_back(grad, unit, inverse):
    inner = jnp.sum(unit * grad, axis=1, keepdims=True)
    return (grad - unit * inner) * inverse


def from_other_core(pair):
    rows = pair.shape[0] // 2
    return pair[pl.ds(pl.multiple_of((1 - lax.axis_index("c")) * rows, rows), rows), :]


def spread_kernel(own, pair, copies):
    rows = own.shape[0]
    first = unit_rows(own[...])[0].astype(jnp.bfloat16)
    second = unit_rows(from_other_core(pair))[0].astype(jnp.bfloat16)
    for peer in range(COLORS):
        copies[peer, :rows, :] = first
        copies[peer, rows:, :] = second


def global_rows(index, is_text, rows):
    bits = rows.bit_length() - 1
    x = lax.axis_index("xh") * 2 + lax.axis_index("xl")
    z = lax.axis_index("zh") * 2 + lax.axis_index("zl")
    low = jnp.minimum(x, 3 - x)
    text = ((lax.axis_index("zl") * 4 + lax.axis_index("xh") * 2) * 2 * 8) * 4 + lax.axis_index("zh")
    image = (lax.axis_index("y") * 8 * 4 + low) * 2 + 1
    place = jnp.where(
        is_text, lax.axis_index("y") + 2 * lax.axis_index("xl"), z + 2 * lax.axis_index("xh")
    )
    first = jnp.where(is_text, text, image) * rows
    per_side = jnp.where(is_text, 64, 2 * (3 - 2 * low)) * rows
    per_slot = jnp.where(is_text, 32, -1) * rows
    per_ring = jnp.where(is_text, 4, 8) * rows

    member = (index >> (bits + 1)) & (COLORS - 1)
    chunk = index >> (bits + 3)
    side = member >> 1
    odd = jnp.where(is_text, lax.axis_index("y") & 1, lax.axis_index("zl"))
    step = chunk ^ (chunk >> 1)
    color = (place + step + ((odd * step) & 1) * 2) & (COLORS - 1)
    ring = (color + ((member & 1) << 2) + (side << 1)) & (RING - 1)
    slot = (index >> bits) & 1
    return first + per_side * side + per_slot * slot + per_ring * ring + (index & (rows - 1))


LOG2_E = 1.4426950408889634


def weigh(rows, scalars, mine, here_start, theirs, there_start):
    speaks_text = lax.axis_index("c") == 0
    slope, offset = -LOG2_E * scalars[0:1, 0:1], -LOG2_E * scalars[0:1, 1:2]
    scores = lax.dot_general(mine, theirs, (((1,), (1,)), ((), ())), preferred_element_type=jnp.float32)
    here_ids = global_rows(
        here_start + lax.broadcasted_iota(jnp.int32, (mine.shape[0], 1), 0), speaks_text, rows
    )
    there_ids = global_rows(
        there_start + lax.broadcasted_iota(jnp.int32, (1, theirs.shape[0]), 1),
        jnp.logical_not(speaks_text),
        rows,
    )
    match = jnp.where(here_ids == there_ids, 1.0, 0.0)
    return (1.0 / (1.0 + jnp.exp2(scores * slope + offset)) - match).astype(jnp.bfloat16)


def weigh_kernel(rows, chunks, count, scalars, *refs):
    mine, theirs, weights = refs[: len(chunks)], refs[len(chunks) : -len(chunks)], refs[-len(chunks) :]
    part = mine[0].shape[0]
    for k in range(len(chunks)):
        for j in range(count):
            weights[k][:, j * part : (j + 1) * part] = weigh(
                rows, scalars, mine[k][...], chunks[k] * part, theirs[j][...], j * part
            )


def tile_kernel(rows, chunks, early, scalars, *refs):
    count = len(chunks)
    mine, ready, theirs, grads = refs[:count], refs[count : -count - 1], refs[-count - 1], refs[-count:]
    part = mine[0].shape[0]
    done = early * part

    def weights_of(k):
        late = weigh(rows, scalars, mine[k][...], chunks[k] * part, theirs[done:, :], done)
        return jnp.concatenate([ready[k][...], late], axis=1) if early else late

    def finish(k, weights):
        grads[k][...] = jnp.dot(weights, theirs[...], preferred_element_type=jnp.float32).astype(
            grads[k].dtype
        )

    before = None
    for k in range(count):
        weights = weights_of(k)
        if k > 0:
            finish(k - 1, before)
        before = weights
    finish(count - 1, before)


def own_member(flip):
    speaks_text = lax.axis_index("c") == 0
    ring = jnp.where(speaks_text, lax.axis_index("y"), lax.axis_index("zh") * 2 + lax.axis_index("zl"))
    side = jnp.where(speaks_text, lax.axis_index("xl"), lax.axis_index("xh")) ^ flip
    low = jnp.where(ring >= 4, 1, 0)
    high = jnp.where(jnp.logical_and(ring >= 2, ring < 6), 2, 3)
    return jnp.where(side == 0, low, high)


def split_kernel(grad, head, tail):
    size = head.shape[0]
    member = own_member(1)
    head[...] = grad[pl.ds(pl.multiple_of(member * size, size), size), :]
    for j in range(1, COLORS):
        start = pl.multiple_of((member ^ j) * size, size)
        tail[(j - 1) * size : j * size, :] = grad[pl.ds(start, size), :]


def merge_kernel(mine, first, second, tail, blocks):
    size = blocks.shape[1]
    member = own_member(0)
    for j in range(COLORS):
        place = pl.ds(pl.multiple_of((member ^ j) * size, size), size)
        total = mine[place, :] + first[place, :].astype(jnp.float32) + second[place, :].astype(jnp.float32)
        if j > 0:
            total = total + tail[(j - 1) * size : j * size, :].astype(jnp.float32)
        blocks[member ^ j] = total.astype(blocks.dtype)


def sum_kernel(parts, head, own, other):
    rows = own.shape[0]
    total = head[...].astype(jnp.float32) + jnp.sum(parts[...].astype(jnp.float32), axis=0)
    own[...] = total[:rows, :]
    other[...] = total[rows:, :]


def finish_kernel(scalars, summed, pair, image, text, grad_image, grad_text):
    speaks_text = lax.axis_index("c") == 0
    scale = scalars[0:1, 0:1]
    own, other = scale * summed[...], scale * from_other_core(pair)
    img_unit, img_inv = unit_rows(image[...])
    txt_unit, txt_inv = unit_rows(text[...])
    grad_image[...] = project_back(jnp.where(speaks_text, other, own), img_unit, img_inv)
    grad_text[...] = project_back(jnp.where(speaks_text, own, other), txt_unit, txt_inv)


VMEM = pl.BlockSpec(memory_space=pltpu.VMEM)
SMALL = pltpu.CompilerParams(vmem_limit_bytes=8 * MIB)
LARGE = pltpu.CompilerParams(vmem_limit_bytes=24 * MIB)


def per_device(image_emb, text_emb, logit_scale, logit_bias):
    rows, width = image_emb.shape
    part = COLORS * 2 * rows
    total = COLORS * part
    scalars = jnp.concatenate([logit_scale, logit_bias]).reshape(1, 2)

    speaks_text = lax.axis_index("c") == 0
    kept = jnp.where(speaks_text, text_emb, image_emb)
    pair = gather_cores(jnp.where(speaks_text, image_emb, text_emb))
    copies = pl.pallas_call(
        spread_kernel,
        out_shape=jax.ShapeDtypeStruct((COLORS, 2 * rows, width), jnp.bfloat16),
        in_specs=[VMEM, VMEM],
        out_specs=VMEM,
        compiler_params=SMALL,
        name="spread",
    )(kept, pair)
    own = exchange(copies).reshape(part, width)
    mine = [own] + [swap_with(own, neighbour) for neighbour in NEIGHBOURS]
    chunks = [swap_cores(chunk) for chunk in mine]
    theirs = jnp.concatenate(chunks, axis=0)
    near, early = (1, 2, 3), 3

    def call(kernel, out_shape, operands, products, name):
        return pl.pallas_call(
            kernel,
            out_shape=out_shape,
            in_specs=[VMEM] * len(operands),
            out_specs=[VMEM] * len(out_shape),
            compiler_params=LARGE,
            cost_estimate=pl.CostEstimate(
                flops=2 * products * part * part * width,
                bytes_accessed=2 * sum(operand.size for operand in operands),
                transcendentals=products * part * part // 2,
            ),
            name=name,
        )(*operands)

    def tile(rows_of, ready, dtype):
        return call(
            lambda *refs: tile_kernel(rows, rows_of, early if ready else 0, *refs),
            [jax.ShapeDtypeStruct((part, width), dtype)] * len(rows_of),
            [scalars, *[mine[chunk] for chunk in rows_of], *ready, theirs],
            len(rows_of) * (8 - (early if ready else 0)),
            "tile",
        )

    ready = call(
        lambda *refs: weigh_kernel(rows, near, early, *refs),
        [jax.ShapeDtypeStruct((part, early * part), jnp.bfloat16)] * len(near),
        [scalars, *[mine[chunk] for chunk in near], *chunks[:early]],
        len(near) * early,
        "weigh",
    )
    size = 2 * rows

    def small_call(kernel, out_shape, operands, name):
        return pl.pallas_call(
            kernel,
            out_shape=out_shape,
            in_specs=[VMEM] * len(operands),
            out_specs=[VMEM] * len(out_shape),
            compiler_params=SMALL,
            name=name,
        )(*operands)

    def half(*shape):
        return jax.ShapeDtypeStruct((*shape, width), jnp.bfloat16)

    blocks = tile(near, ready, jnp.bfloat16)
    late, tail = small_call(split_kernel, [half(size), half(part - size)], [blocks[2]], "split")
    first, second, tail = [
        swap_with(block, neighbour) for block, neighbour in zip((blocks[0], blocks[1], tail), NEIGHBOURS)
    ]
    head = swap_with(late, NEIGHBOURS[2])
    (summed,) = tile((0,), [], jnp.float32)
    (merged,) = small_call(merge_kernel, [half(COLORS, size)], [summed, first, second, tail], "merge")
    out = jax.ShapeDtypeStruct((rows, width), jnp.float32)
    own, other = small_call(sum_kernel, [out, out], [exchange(merged), head], "sum")
    return pl.pallas_call(
        finish_kernel,
        out_shape=(out, out),
        in_specs=[VMEM] * 5,
        out_specs=(VMEM, VMEM),
        compiler_params=SMALL,
        name="finish",
    )(scalars, own, gather_cores(other), image_emb, text_emb)


def solution(mesh):
    fine = Mesh(mesh.devices.reshape(SHAPE), NAMES)
    return jax.shard_map(
        per_device,
        mesh=fine,
        in_specs=(P(IMG_ORDER, None), P(TXT_ORDER, None), P(), P()),
        out_specs=(P(IMG_ORDER, None), P(TXT_ORDER, None)),
        check_vma=False,
    )
```

```python
import jax
import jax.numpy as jnp
from jax import lax
from jax.experimental import pallas as pl
from jax.experimental.pallas import tpu as pltpu
from jax.sharding import Mesh, PartitionSpec as P

EPS = 1e-06
NAMES = ("zl", "xh", "xl", "c", "y", "zh")
SHAPE = (2, 2, 2, 2, 8, 4)
IMG_ORDER = ("y", "zh", "zl", "xh", "xl", "c")
TXT_ORDER = ("zl", "xh", "xl", "c", "y", "zh")
RING = 8
COLORS = 4
MIB = 1 << 20


def device_index(x, y, z, c):
    return ((((z % 2) * 4 + x) * 2 + c) * 8 + y) * 4 + z // 2


def speaker(kind, line, pair, ring, side):
    if kind == 0:
        return device_index(2 * pair + side, ring % RING, line, 0)
    return device_index(3 - pair if side else pair, line, ring % RING, 1)


def lines():
    return [(kind, line, pair) for kind in (0, 1) for line in range(RING) for pair in (0, 1)]


def color_groups():
    return [
        [speaker(*line, color + ring, side) for ring, side in ((0, 0), (4, 0), (2, 1), (6, 1))]
        for line in lines()
        for color in range(COLORS)
    ]


NEIGHBOURS = (
    lambda ring, side: (ring ^ 1, side),
    lambda ring, side: (((ring + 1) ^ 1) - 1, side),
    lambda ring, side: (ring, 1 - side),
)


def swap_with(block, neighbour):
    pairs = [
        (speaker(*line, *neighbour(ring, side)), speaker(*line, ring, side))
        for line in lines()
        for ring in range(RING)
        for side in (0, 1)
    ]
    return lax.ppermute(block, NAMES, pairs)


def exchange(blocks):
    return lax.all_to_all(blocks, NAMES, 0, 0, axis_index_groups=color_groups(), tiled=False)


def swap_cores(block):
    return lax.ppermute(block, "c", [(0, 1), (1, 0)])


def gather_cores(block):
    return lax.all_gather(block, "c", axis=0, tiled=True)


def unit_rows(embedded):
    values = embedded.astype(jnp.float32)
    inverse = lax.rsqrt(jnp.sum(values * values, axis=1, keepdims=True) + EPS)
    return (values * inverse, inverse)


def project_back(grad, unit, inverse):
    inner = jnp.sum(unit * grad, axis=1, keepdims=True)
    return (grad - unit * inner) * inverse


def from_other_core(pair):
    rows = pair.shape[0] // 2
    return pair[pl.ds(pl.multiple_of((1 - lax.axis_index("c")) * rows, rows), rows), :]


def spread_kernel(own, pair, copies, block):
    rows = own.shape[0]
    first = unit_rows(own[...])[0].astype(jnp.bfloat16)
    second = unit_rows(from_other_core(pair))[0].astype(jnp.bfloat16)
    for member in range(COLORS):
        copies[member, :rows, :] = first
        copies[member, rows:, :] = second
    block[:rows, :] = first
    block[rows:, :] = second


def own_node(is_text):
    ring = jnp.where(is_text, lax.axis_index("y"), lax.axis_index("zh") * 2 + lax.axis_index("zl"))
    side = jnp.where(is_text, lax.axis_index("xl"), lax.axis_index("xh"))
    return ring, side


def own_member():
    ring, side = own_node(lax.axis_index("c") == 0)
    low = jnp.where(ring >= 4, 1, 0)
    high = jnp.where(jnp.logical_and(ring >= 2, ring < 6), 2, 3)
    return jnp.where(side == 0, low, high)


def order_kernel(gathered, block, rest):
    size = gathered.shape[1]
    member = own_member()
    for j in range(COLORS):
        rows = gathered[member ^ j]
        block[j * size : (j + 1) * size, :] = rows
        if j > 0:
            rest[(j - 1) * size : j * size, :] = rows


def global_rows(index, is_text, rows):
    bits = rows.bit_length() - 1
    x = lax.axis_index("xh") * 2 + lax.axis_index("xl")
    low = jnp.minimum(x, 3 - x)
    text = ((lax.axis_index("zl") * 4 + lax.axis_index("xh") * 2) * 2 * 8) * 4 + lax.axis_index("zh")
    image = (lax.axis_index("y") * 8 * 4 + low) * 2 + 1
    own_ring, own_side = own_node(is_text)
    first = jnp.where(is_text, text, image) * rows
    per_side = jnp.where(is_text, 64, 2 * (3 - 2 * low)) * rows
    per_slot = jnp.where(is_text, 32, -1) * rows
    per_ring = jnp.where(is_text, 4, 8) * rows

    member = (index >> (bits + 1)) & (COLORS - 1)
    chunk = index >> (bits + 3)
    node_ring = jnp.where(
        chunk == 1, own_ring ^ 1, jnp.where(chunk == 2, ((own_ring + 1) ^ 1) - 1, own_ring)
    )
    node_side = jnp.where(chunk == 3, 1 - own_side, own_side)
    turn = member >> 1
    side = node_side ^ turn
    ring = (node_ring + 4 * (member & 1) + 2 * (1 - 2 * node_side) * turn) & (RING - 1)
    slot = (index >> bits) & 1
    return first + per_side * side + per_slot * slot + per_ring * ring + (index & (rows - 1))


LOG2_E = 1.4426950408889634


def weigh(rows, scalars, mine, here_start, theirs, there_start):
    speaks_text = lax.axis_index("c") == 0
    slope, offset = -LOG2_E * scalars[0:1, 0:1], -LOG2_E * scalars[0:1, 1:2]
    scores = lax.dot_general(mine, theirs, (((1,), (1,)), ((), ())), preferred_element_type=jnp.float32)
    here_ids = global_rows(
        here_start + lax.broadcasted_iota(jnp.int32, (mine.shape[0], 1), 0), speaks_text, rows
    )
    there_ids = global_rows(
        there_start + lax.broadcasted_iota(jnp.int32, (1, theirs.shape[0]), 1),
        jnp.logical_not(speaks_text),
        rows,
    )
    match = jnp.where(here_ids == there_ids, 1.0, 0.0)
    return (1.0 / (1.0 + jnp.exp2(scores * slope + offset)) - match).astype(jnp.bfloat16)


def weigh_kernel(rows, chunks, count, scalars, *refs):
    mine, theirs, weights = refs[: len(chunks)], refs[len(chunks) : -len(chunks)], refs[-len(chunks) :]
    part = mine[0].shape[0]
    for k in range(len(chunks)):
        for j in range(count):
            weights[k][:, j * part : (j + 1) * part] = weigh(
                rows, scalars, mine[k][...], chunks[k] * part, theirs[j][...], j * part
            )


def tile_kernel(rows, chunks, early, scalars, *refs):
    count = len(chunks)
    mine, ready, theirs, grads = refs[:count], refs[count : -count - 1], refs[-count - 1], refs[-count:]
    part = mine[0].shape[0]
    done = early * part

    def weights_of(k):
        late = weigh(rows, scalars, mine[k][...], chunks[k] * part, theirs[done:, :], done)
        return jnp.concatenate([ready[k][...], late], axis=1) if early else late

    def finish(k, weights):
        grads[k][...] = jnp.dot(weights, theirs[...], preferred_element_type=jnp.float32).astype(
            grads[k].dtype
        )

    before = None
    for k in range(count):
        weights = weights_of(k)
        if k > 0:
            finish(k - 1, before)
        before = weights
    finish(count - 1, before)


def merge_kernel(mine, first, second, tail, blocks):
    size = blocks.shape[1]
    member = own_member()
    for j in range(COLORS):
        place = slice(j * size, (j + 1) * size)
        total = mine[place, :] + first[place, :].astype(jnp.float32) + second[place, :].astype(jnp.float32)
        if j > 0:
            total = total + tail[(j - 1) * size : j * size, :].astype(jnp.float32)
        blocks[member ^ j] = total.astype(blocks.dtype)


def sum_kernel(parts, head, own, other):
    rows = own.shape[0]
    total = head[...].astype(jnp.float32) + jnp.sum(parts[...].astype(jnp.float32), axis=0)
    own[...] = total[:rows, :]
    other[...] = total[rows:, :]


def finish_kernel(scalars, summed, pair, image, text, grad_image, grad_text):
    speaks_text = lax.axis_index("c") == 0
    scale = scalars[0:1, 0:1]
    own, other = scale * summed[...], scale * from_other_core(pair)
    img_unit, img_inv = unit_rows(image[...])
    txt_unit, txt_inv = unit_rows(text[...])
    grad_image[...] = project_back(jnp.where(speaks_text, other, own), img_unit, img_inv)
    grad_text[...] = project_back(jnp.where(speaks_text, own, other), txt_unit, txt_inv)


VMEM = pl.BlockSpec(memory_space=pltpu.VMEM)
SMALL = pltpu.CompilerParams(vmem_limit_bytes=8 * MIB)
LARGE = pltpu.CompilerParams(vmem_limit_bytes=24 * MIB)


def per_device(image_emb, text_emb, logit_scale, logit_bias):
    rows, width = image_emb.shape
    part = COLORS * 2 * rows
    total = COLORS * part
    scalars = jnp.concatenate([logit_scale, logit_bias]).reshape(1, 2)

    speaks_text = lax.axis_index("c") == 0
    kept = jnp.where(speaks_text, text_emb, image_emb)
    pair = gather_cores(jnp.where(speaks_text, image_emb, text_emb))
    size = 2 * rows
    spread = jax.ShapeDtypeStruct((COLORS, size, width), jnp.bfloat16)

    def small_call(kernel, out_shape, operands, name):
        return pl.pallas_call(
            kernel,
            out_shape=out_shape,
            in_specs=[VMEM] * len(operands),
            out_specs=[VMEM] * len(out_shape),
            compiler_params=SMALL,
            name=name,
        )(*operands)

    def half(count):
        return jax.ShapeDtypeStruct((count, width), jnp.bfloat16)

    copies, block = small_call(spread_kernel, [spread, half(size)], [kept, pair], "spread")
    heads = [swap_with(block, neighbour) for neighbour in NEIGHBOURS]
    own, rest = small_call(order_kernel, [half(part), half(part - size)], [exchange(copies)], "order")
    mine = [own] + [
        jnp.concatenate([head, swap_with(rest, neighbour)], axis=0)
        for head, neighbour in zip(heads, NEIGHBOURS)
    ]
    chunks = [swap_cores(chunk) for chunk in mine]
    theirs = jnp.concatenate(chunks, axis=0)
    near, early = (1, 2, 3), 3

    def call(kernel, out_shape, operands, products, name):
        return pl.pallas_call(
            kernel,
            out_shape=out_shape,
            in_specs=[VMEM] * len(operands),
            out_specs=[VMEM] * len(out_shape),
            compiler_params=LARGE,
            cost_estimate=pl.CostEstimate(
                flops=2 * products * part * part * width,
                bytes_accessed=2 * sum(operand.size for operand in operands),
                transcendentals=products * part * part // 2,
            ),
            name=name,
        )(*operands)

    def tile(rows_of, ready, dtype):
        return call(
            lambda *refs: tile_kernel(rows, rows_of, early if ready else 0, *refs),
            [jax.ShapeDtypeStruct((part, width), dtype)] * len(rows_of),
            [scalars, *[mine[chunk] for chunk in rows_of], *ready, theirs],
            len(rows_of) * (8 - (early if ready else 0)),
            "tile",
        )

    ready = call(
        lambda *refs: weigh_kernel(rows, near, early, *refs),
        [jax.ShapeDtypeStruct((part, early * part), jnp.bfloat16)] * len(near),
        [scalars, *[mine[chunk] for chunk in near], *chunks[:early]],
        len(near) * early,
        "weigh",
    )
    blocks = tile(near, ready, jnp.bfloat16)
    first, second, tail = [
        swap_with(block, neighbour)
        for block, neighbour in zip((blocks[0], blocks[1], blocks[2][size:]), NEIGHBOURS)
    ]
    head = swap_with(blocks[2][:size], NEIGHBOURS[2])
    (summed,) = tile((0,), [], jnp.float32)
    (merged,) = small_call(merge_kernel, [spread], [summed, first, second, tail], "merge")
    out = jax.ShapeDtypeStruct((rows, width), jnp.float32)
    own, other = small_call(sum_kernel, [out, out], [exchange(merged), head], "sum")
    return pl.pallas_call(
        finish_kernel,
        out_shape=(out, out),
        in_specs=[VMEM] * 5,
        out_specs=(VMEM, VMEM),
        compiler_params=SMALL,
        name="finish",
    )(scalars, own, gather_cores(other), image_emb, text_emb)


def solution(mesh):
    fine = Mesh(mesh.devices.reshape(SHAPE), NAMES)
    return jax.shard_map(
        per_device,
        mesh=fine,
        in_specs=(P(IMG_ORDER, None), P(TXT_ORDER, None), P(), P()),
        out_specs=(P(IMG_ORDER, None), P(TXT_ORDER, None)),
        check_vma=False,
    )
```

```python
import jax
import jax.numpy as jnp
from jax import lax
from jax.experimental import pallas as pl
from jax.experimental.pallas import tpu as pltpu
from jax.sharding import Mesh, PartitionSpec as P

EPS = 1e-06
NAMES = ("zl", "xh", "xl", "c", "y", "zh")
SHAPE = (2, 2, 2, 2, 8, 4)
IMG_ORDER = ("y", "zh", "zl", "xh", "xl", "c")
TXT_ORDER = ("zl", "xh", "xl", "c", "y", "zh")
RING = 8
COLORS = 4
MIB = 1 << 20


def device_index(x, y, z, c):
    return ((((z % 2) * 4 + x) * 2 + c) * 8 + y) * 4 + z // 2


def speaker(kind, line, pair, ring, side):
    if kind == 0:
        return device_index(2 * pair + side, ring % RING, line, 0)
    return device_index(3 - pair if side else pair, line, ring % RING, 1)


def lines():
    return [(kind, line, pair) for kind in (0, 1) for line in range(RING) for pair in (0, 1)]


def color_groups():
    return [
        [speaker(*line, color + ring, side) for ring, side in ((0, 0), (4, 0), (2, 1), (6, 1))]
        for line in lines()
        for color in range(COLORS)
    ]


NEIGHBOURS = (
    lambda ring, side: (ring ^ 1, side),
    lambda ring, side: (((ring + 1) ^ 1) - 1, side),
    lambda ring, side: (ring, 1 - side),
)


def swap_with(block, neighbour):
    pairs = [
        (speaker(*line, *neighbour(ring, side)), speaker(*line, ring, side))
        for line in lines()
        for ring in range(RING)
        for side in (0, 1)
    ]
    return lax.ppermute(block, NAMES, pairs)


def exchange(blocks):
    return lax.all_to_all(blocks, NAMES, 0, 0, axis_index_groups=color_groups(), tiled=False)


def swap_cores(block):
    return lax.ppermute(block, "c", [(0, 1), (1, 0)])


def gather_cores(block):
    return lax.all_gather(block, "c", axis=0, tiled=True)


def unit_rows(embedded):
    values = embedded.astype(jnp.float32)
    inverse = lax.rsqrt(jnp.sum(values * values, axis=1, keepdims=True) + EPS)
    return (values * inverse, inverse)


def project_back(grad, unit, inverse):
    inner = jnp.sum(unit * grad, axis=1, keepdims=True)
    return (grad - unit * inner) * inverse


def from_other_core(pair):
    rows = pair.shape[0] // 2
    return pair[pl.ds(pl.multiple_of((1 - lax.axis_index("c")) * rows, rows), rows), :]


def spread_kernel(own, pair, copies, block):
    rows = own.shape[0]
    first = unit_rows(own[...])[0].astype(jnp.bfloat16)
    second = unit_rows(from_other_core(pair))[0].astype(jnp.bfloat16)
    for member in range(COLORS):
        copies[member, :rows, :] = first
        copies[member, rows:, :] = second
    block[:rows, :] = first
    block[rows:, :] = second


def own_node(is_text):
    ring = jnp.where(is_text, lax.axis_index("y"), lax.axis_index("zh") * 2 + lax.axis_index("zl"))
    side = jnp.where(is_text, lax.axis_index("xl"), lax.axis_index("xh"))
    return ring, side


def own_member():
    ring, side = own_node(lax.axis_index("c") == 0)
    low = jnp.where(ring >= 4, 1, 0)
    high = jnp.where(jnp.logical_and(ring >= 2, ring < 6), 2, 3)
    return jnp.where(side == 0, low, high)


def order_kernel(gathered, block, rest):
    size = gathered.shape[1]
    member = own_member()
    for j in range(COLORS):
        rows = gathered[member ^ j]
        block[j * size : (j + 1) * size, :] = rows
        if j > 0:
            rest[(j - 1) * size : j * size, :] = rows


def global_rows(index, is_text, rows):
    bits = rows.bit_length() - 1
    x = lax.axis_index("xh") * 2 + lax.axis_index("xl")
    low = jnp.minimum(x, 3 - x)
    text = ((lax.axis_index("zl") * 4 + lax.axis_index("xh") * 2) * 2 * 8) * 4 + lax.axis_index("zh")
    image = (lax.axis_index("y") * 8 * 4 + low) * 2 + 1
    own_ring, own_side = own_node(is_text)
    first = jnp.where(is_text, text, image) * rows
    per_side = jnp.where(is_text, 64, 2 * (3 - 2 * low)) * rows
    per_slot = jnp.where(is_text, 32, -1) * rows
    per_ring = jnp.where(is_text, 4, 8) * rows

    member = (index >> (bits + 1)) & (COLORS - 1)
    chunk = index >> (bits + 3)
    node_ring = jnp.where(
        chunk == 1, own_ring ^ 1, jnp.where(chunk == 2, ((own_ring + 1) ^ 1) - 1, own_ring)
    )
    node_side = jnp.where(chunk == 3, 1 - own_side, own_side)
    turn = member >> 1
    side = node_side ^ turn
    ring = (node_ring + 4 * (member & 1) + 2 * (1 - 2 * node_side) * turn) & (RING - 1)
    slot = (index >> bits) & 1
    return first + per_side * side + per_slot * slot + per_ring * ring + (index & (rows - 1))


LOG2_E = 1.4426950408889634


def weigh(rows, scalars, mine, here_start, theirs, there_start):
    speaks_text = lax.axis_index("c") == 0
    slope, offset = -LOG2_E * scalars[0:1, 0:1], -LOG2_E * scalars[0:1, 1:2]
    scores = lax.dot_general(mine, theirs, (((1,), (1,)), ((), ())), preferred_element_type=jnp.float32)
    here_ids = global_rows(
        here_start + lax.broadcasted_iota(jnp.int32, (mine.shape[0], 1), 0), speaks_text, rows
    )
    there_ids = global_rows(
        there_start + lax.broadcasted_iota(jnp.int32, (1, theirs.shape[0]), 1),
        jnp.logical_not(speaks_text),
        rows,
    )
    match = jnp.where(here_ids == there_ids, 1.0, 0.0)
    return (1.0 / (1.0 + jnp.exp2(scores * slope + offset)) - match).astype(jnp.bfloat16)


def weigh_kernel(rows, chunks, count, scalars, *refs):
    mine, theirs, weights = refs[: len(chunks)], refs[len(chunks) : -len(chunks)], refs[-len(chunks) :]
    part = mine[0].shape[0]
    for k in range(len(chunks)):
        for j in range(count):
            weights[k][:, j * part : (j + 1) * part] = weigh(
                rows, scalars, mine[k][...], chunks[k] * part, theirs[j][...], j * part
            )


def tile_kernel(rows, chunks, early, scalars, *refs):
    count = len(chunks)
    mine, ready, theirs, grads = refs[:count], refs[count : -count - 1], refs[-count - 1], refs[-count:]
    part = mine[0].shape[0]
    done = early * part

    def weights_of(k):
        late = weigh(rows, scalars, mine[k][...], chunks[k] * part, theirs[done:, :], done)
        return jnp.concatenate([ready[k][...], late], axis=1) if early else late

    def finish(k, weights):
        grads[k][...] = jnp.dot(weights, theirs[...], preferred_element_type=jnp.float32).astype(
            grads[k].dtype
        )

    before = None
    for k in range(count):
        weights = weights_of(k)
        if k > 0:
            finish(k - 1, before)
        before = weights
    finish(count - 1, before)


def merge_kernel(mine, first, second, tail, blocks):
    size = blocks.shape[1]
    member = own_member()
    for j in range(COLORS):
        place = slice(j * size, (j + 1) * size)
        total = mine[place, :] + first[place, :].astype(jnp.float32) + second[place, :].astype(jnp.float32)
        if j > 0:
            total = total + tail[(j - 1) * size : j * size, :].astype(jnp.float32)
        blocks[member ^ j] = total.astype(blocks.dtype)


def sum_kernel(parts, head, own, other):
    rows = own.shape[0]
    total = head[...].astype(jnp.float32) + jnp.sum(parts[...].astype(jnp.float32), axis=0)
    own[...] = total[:rows, :]
    other[...] = total[rows:, :]


def unit_kernel(image, text, img_unit, txt_unit, img_inv, txt_inv):
    img_unit[...], img_inv[...] = unit_rows(image[...])
    txt_unit[...], txt_inv[...] = unit_rows(text[...])


def finish_kernel(scalars, summed, pair, img_unit, txt_unit, img_inv, txt_inv, grad_image, grad_text):
    speaks_text = lax.axis_index("c") == 0
    scale = scalars[0:1, 0:1]
    own, other = scale * summed[...], scale * from_other_core(pair)
    grad_image[...] = project_back(jnp.where(speaks_text, other, own), img_unit[...], img_inv[...])
    grad_text[...] = project_back(jnp.where(speaks_text, own, other), txt_unit[...], txt_inv[...])


VMEM = pl.BlockSpec(memory_space=pltpu.VMEM)
SMALL = pltpu.CompilerParams(vmem_limit_bytes=8 * MIB)
LARGE = pltpu.CompilerParams(vmem_limit_bytes=24 * MIB)


def per_device(image_emb, text_emb, logit_scale, logit_bias):
    rows, width = image_emb.shape
    part = COLORS * 2 * rows
    total = COLORS * part
    scalars = jnp.concatenate([logit_scale, logit_bias]).reshape(1, 2)

    speaks_text = lax.axis_index("c") == 0
    kept = jnp.where(speaks_text, text_emb, image_emb)
    pair = gather_cores(jnp.where(speaks_text, image_emb, text_emb))
    size = 2 * rows
    spread = jax.ShapeDtypeStruct((COLORS, size, width), jnp.bfloat16)

    def small_call(kernel, out_shape, operands, name):
        return pl.pallas_call(
            kernel,
            out_shape=out_shape,
            in_specs=[VMEM] * len(operands),
            out_specs=[VMEM] * len(out_shape),
            compiler_params=SMALL,
            name=name,
        )(*operands)

    def half(count):
        return jax.ShapeDtypeStruct((count, width), jnp.bfloat16)

    copies, block = small_call(spread_kernel, [spread, half(size)], [kept, pair], "spread")
    heads = [swap_with(block, neighbour) for neighbour in NEIGHBOURS]
    own, rest = small_call(order_kernel, [half(part), half(part - size)], [exchange(copies)], "order")
    mine = [own] + [
        jnp.concatenate([head, swap_with(rest, neighbour)], axis=0)
        for head, neighbour in zip(heads, NEIGHBOURS)
    ]
    chunks = [swap_cores(chunk) for chunk in mine]
    theirs = jnp.concatenate(chunks, axis=0)
    near, early = (1, 2, 3), 3

    def call(kernel, out_shape, operands, products, name):
        return pl.pallas_call(
            kernel,
            out_shape=out_shape,
            in_specs=[VMEM] * len(operands),
            out_specs=[VMEM] * len(out_shape),
            compiler_params=LARGE,
            cost_estimate=pl.CostEstimate(
                flops=2 * products * part * part * width,
                bytes_accessed=2 * sum(operand.size for operand in operands),
                transcendentals=products * part * part // 2,
            ),
            name=name,
        )(*operands)

    def tile(rows_of, ready, dtype):
        return call(
            lambda *refs: tile_kernel(rows, rows_of, early if ready else 0, *refs),
            [jax.ShapeDtypeStruct((part, width), dtype)] * len(rows_of),
            [scalars, *[mine[chunk] for chunk in rows_of], *ready, theirs],
            len(rows_of) * (8 - (early if ready else 0)),
            "tile",
        )

    ready = call(
        lambda *refs: weigh_kernel(rows, near, early, *refs),
        [jax.ShapeDtypeStruct((part, early * part), jnp.bfloat16)] * len(near),
        [scalars, *[mine[chunk] for chunk in near], *chunks[:early]],
        len(near) * early,
        "weigh",
    )
    blocks = tile(near, ready, jnp.bfloat16)
    first, second, tail = [
        swap_with(block, neighbour)
        for block, neighbour in zip((blocks[0], blocks[1], blocks[2][size:]), NEIGHBOURS)
    ]
    head = swap_with(blocks[2][:size], NEIGHBOURS[2])
    full = jax.ShapeDtypeStruct((rows, width), jnp.float32)
    column = jax.ShapeDtypeStruct((rows, 1), jnp.float32)
    units = small_call(unit_kernel, [full, full, column, column], [image_emb, text_emb], "units")
    mine[0], units = lax.optimization_barrier((mine[0], units))
    (summed,) = tile((0,), [], jnp.float32)
    (merged,) = small_call(merge_kernel, [spread], [summed, first, second, tail], "merge")
    out = jax.ShapeDtypeStruct((rows, width), jnp.float32)
    own, other = small_call(sum_kernel, [out, out], [exchange(merged), head], "sum")
    operands = [scalars, own, gather_cores(other), *units]
    return tuple(small_call(finish_kernel, [out, out], operands, "finish"))


def solution(mesh):
    fine = Mesh(mesh.devices.reshape(SHAPE), NAMES)
    return jax.shard_map(
        per_device,
        mesh=fine,
        in_specs=(P(IMG_ORDER, None), P(TXT_ORDER, None), P(), P()),
        out_specs=(P(IMG_ORDER, None), P(TXT_ORDER, None)),
        check_vma=False,
    )
```

```python
import jax
import jax.numpy as jnp
from jax import lax
from jax.experimental import pallas as pl
from jax.experimental.pallas import tpu as pltpu
from jax.sharding import Mesh, PartitionSpec as P

EPS = 1e-06
NAMES = ("zl", "xh", "xl", "c", "y", "zh")
SHAPE = (2, 2, 2, 2, 8, 4)
IMG_ORDER = ("y", "zh", "zl", "xh", "xl", "c")
TXT_ORDER = ("zl", "xh", "xl", "c", "y", "zh")
RING = 8
COLORS = 4
MIB = 1 << 20


def device_index(x, y, z, c):
    return ((((z % 2) * 4 + x) * 2 + c) * 8 + y) * 4 + z // 2


def speaker(kind, line, pair, ring, side):
    if kind == 0:
        return device_index(2 * pair + side, ring % RING, line, 0)
    return device_index(3 - pair if side else pair, line, ring % RING, 1)


def lines():
    return [(kind, line, pair) for kind in (0, 1) for line in range(RING) for pair in (0, 1)]


def color_groups():
    return [
        [speaker(*line, color + ring, side) for ring, side in ((0, 0), (4, 0), (2, 1), (6, 1))]
        for line in lines()
        for color in range(COLORS)
    ]


NEIGHBOURS = (
    lambda ring, side: (ring ^ 1, side),
    lambda ring, side: (((ring + 1) ^ 1) - 1, side),
    lambda ring, side: (ring, 1 - side),
)


def swap_with(block, neighbour):
    pairs = [
        (speaker(*line, *neighbour(ring, side)), speaker(*line, ring, side))
        for line in lines()
        for ring in range(RING)
        for side in (0, 1)
    ]
    return lax.ppermute(block, NAMES, pairs)


def exchange(blocks):
    return lax.all_to_all(blocks, NAMES, 0, 0, axis_index_groups=color_groups(), tiled=False)


def swap_cores(block):
    return lax.ppermute(block, "c", [(0, 1), (1, 0)])


def gather_cores(block):
    return lax.all_gather(block, "c", axis=0, tiled=True)


def unit_rows(embedded):
    values = embedded.astype(jnp.float32)
    inverse = lax.rsqrt(jnp.sum(values * values, axis=1, keepdims=True) + EPS)
    return (values * inverse, inverse)


def project_back(grad, unit, inverse):
    inner = jnp.sum(unit * grad, axis=1, keepdims=True)
    return (grad - unit * inner) * inverse


def from_other_core(pair):
    rows = pair.shape[0] // 2
    return pair[pl.ds(pl.multiple_of((1 - lax.axis_index("c")) * rows, rows), rows), :]


def spread_kernel(own, pair, copies, block):
    rows = own.shape[0]
    first = unit_rows(own[...])[0].astype(jnp.bfloat16)
    second = unit_rows(from_other_core(pair))[0].astype(jnp.bfloat16)
    for member in range(COLORS):
        copies[member, :rows, :] = first
        copies[member, rows:, :] = second
    block[:rows, :] = first
    block[rows:, :] = second


def own_node(is_text):
    ring = jnp.where(is_text, lax.axis_index("y"), lax.axis_index("zh") * 2 + lax.axis_index("zl"))
    side = jnp.where(is_text, lax.axis_index("xl"), lax.axis_index("xh"))
    return ring, side


def own_member():
    ring, side = own_node(lax.axis_index("c") == 0)
    low = jnp.where(ring >= 4, 1, 0)
    high = jnp.where(jnp.logical_and(ring >= 2, ring < 6), 2, 3)
    return jnp.where(side == 0, low, high)


def order_kernel(gathered, block, rest):
    size = gathered.shape[1]
    member = own_member()
    for j in range(COLORS):
        rows = gathered[member ^ j]
        block[j * size : (j + 1) * size, :] = rows
        if j > 0:
            rest[(j - 1) * size : j * size, :] = rows


def global_rows(index, is_text, rows):
    bits = rows.bit_length() - 1
    x = lax.axis_index("xh") * 2 + lax.axis_index("xl")
    low = jnp.minimum(x, 3 - x)
    text = ((lax.axis_index("zl") * 4 + lax.axis_index("xh") * 2) * 2 * 8) * 4 + lax.axis_index("zh")
    image = (lax.axis_index("y") * 8 * 4 + low) * 2 + 1
    own_ring, own_side = own_node(is_text)
    first = jnp.where(is_text, text, image) * rows
    per_side = jnp.where(is_text, 64, 2 * (3 - 2 * low)) * rows
    per_slot = jnp.where(is_text, 32, -1) * rows
    per_ring = jnp.where(is_text, 4, 8) * rows

    member = (index >> (bits + 1)) & (COLORS - 1)
    chunk = index >> (bits + 3)
    node_ring = jnp.where(
        chunk == 1, own_ring ^ 1, jnp.where(chunk == 2, ((own_ring + 1) ^ 1) - 1, own_ring)
    )
    node_side = jnp.where(chunk == 3, 1 - own_side, own_side)
    turn = member >> 1
    side = node_side ^ turn
    ring = (node_ring + 4 * (member & 1) + 2 * (1 - 2 * node_side) * turn) & (RING - 1)
    slot = (index >> bits) & 1
    return first + per_side * side + per_slot * slot + per_ring * ring + (index & (rows - 1))


LOG2_E = 1.4426950408889634


def weigh(rows, scalars, mine, here_start, theirs, there_start):
    speaks_text = lax.axis_index("c") == 0
    slope, offset = -LOG2_E * scalars[0:1, 0:1], -LOG2_E * scalars[0:1, 1:2]
    scores = lax.dot_general(mine, theirs, (((1,), (1,)), ((), ())), preferred_element_type=jnp.float32)
    here_ids = global_rows(
        here_start + lax.broadcasted_iota(jnp.int32, (mine.shape[0], 1), 0), speaks_text, rows
    )
    there_ids = global_rows(
        there_start + lax.broadcasted_iota(jnp.int32, (1, theirs.shape[0]), 1),
        jnp.logical_not(speaks_text),
        rows,
    )
    match = jnp.where(here_ids == there_ids, 1.0, 0.0)
    return (1.0 / (1.0 + jnp.exp2(scores * slope + offset)) - match).astype(jnp.bfloat16)


def weigh_kernel(rows, chunks, count, scalars, *refs):
    mine, theirs, weights = refs[: len(chunks)], refs[len(chunks) : -len(chunks)], refs[-len(chunks) :]
    part = mine[0].shape[0]
    for k in range(len(chunks)):
        for j in range(count):
            weights[k][:, j * part : (j + 1) * part] = weigh(
                rows, scalars, mine[k][...], chunks[k] * part, theirs[j][...], j * part
            )


def tile_kernel(rows, chunks, early, scalars, *refs):
    count = len(chunks)
    mine, ready, theirs, grads = refs[:count], refs[count : -count - 1], refs[-count - 1], refs[-count:]
    part = mine[0].shape[0]
    done = early * part

    def weights_of(k):
        late = weigh(rows, scalars, mine[k][...], chunks[k] * part, theirs[done:, :], done)
        return jnp.concatenate([ready[k][...], late], axis=1) if early else late

    def finish(k, weights):
        grads[k][...] = jnp.dot(weights, theirs[...], preferred_element_type=jnp.float32).astype(
            grads[k].dtype
        )

    before = None
    for k in range(count):
        weights = weights_of(k)
        if k > 0:
            finish(k - 1, before)
        before = weights
    finish(count - 1, before)


def merge_kernel(mine, first, second, tail, blocks):
    size = blocks.shape[1]
    member = own_member()
    blocks[member] = jnp.zeros(blocks.shape[1:], blocks.dtype)
    for j in range(1, COLORS):
        place = slice(j * size, (j + 1) * size)
        total = mine[place, :] + first[place, :].astype(jnp.float32) + second[place, :].astype(jnp.float32)
        total = total + tail[(j - 1) * size : j * size, :].astype(jnp.float32)
        blocks[member ^ j] = total.astype(blocks.dtype)


def sum_kernel(parts, mine, first, second, head, own, other):
    rows = own.shape[0]
    size = parts.shape[1]
    total = mine[:size, :] + jnp.sum(parts[...].astype(jnp.float32), axis=0)
    for received in (first, second, head):
        total = total + received[:size, :].astype(jnp.float32)
    own[...] = total[:rows, :]
    other[...] = total[rows:, :]


def unit_kernel(image, text, img_unit, txt_unit, img_inv, txt_inv):
    img_unit[...], img_inv[...] = unit_rows(image[...])
    txt_unit[...], txt_inv[...] = unit_rows(text[...])


def finish_kernel(scalars, summed, pair, img_unit, txt_unit, img_inv, txt_inv, grad_image, grad_text):
    speaks_text = lax.axis_index("c") == 0
    scale = scalars[0:1, 0:1]
    own, other = scale * summed[...], scale * from_other_core(pair)
    grad_image[...] = project_back(jnp.where(speaks_text, other, own), img_unit[...], img_inv[...])
    grad_text[...] = project_back(jnp.where(speaks_text, own, other), txt_unit[...], txt_inv[...])


VMEM = pl.BlockSpec(memory_space=pltpu.VMEM)
SMALL = pltpu.CompilerParams(vmem_limit_bytes=8 * MIB)
LARGE = pltpu.CompilerParams(vmem_limit_bytes=24 * MIB)


def per_device(image_emb, text_emb, logit_scale, logit_bias):
    rows, width = image_emb.shape
    part = COLORS * 2 * rows
    total = COLORS * part
    scalars = jnp.concatenate([logit_scale, logit_bias]).reshape(1, 2)

    speaks_text = lax.axis_index("c") == 0
    kept = jnp.where(speaks_text, text_emb, image_emb)
    pair = gather_cores(jnp.where(speaks_text, image_emb, text_emb))
    size = 2 * rows
    spread = jax.ShapeDtypeStruct((COLORS, size, width), jnp.bfloat16)

    def small_call(kernel, out_shape, operands, name):
        return pl.pallas_call(
            kernel,
            out_shape=out_shape,
            in_specs=[VMEM] * len(operands),
            out_specs=[VMEM] * len(out_shape),
            compiler_params=SMALL,
            name=name,
        )(*operands)

    def half(count):
        return jax.ShapeDtypeStruct((count, width), jnp.bfloat16)

    copies, block = small_call(spread_kernel, [spread, half(size)], [kept, pair], "spread")
    heads = [swap_with(block, neighbour) for neighbour in NEIGHBOURS]
    own, rest = small_call(order_kernel, [half(part), half(part - size)], [exchange(copies)], "order")
    mine = [own] + [
        jnp.concatenate([head, swap_with(rest, neighbour)], axis=0)
        for head, neighbour in zip(heads, NEIGHBOURS)
    ]
    chunks = [swap_cores(chunk) for chunk in mine]
    theirs = jnp.concatenate(chunks, axis=0)
    near, early = (1, 2, 3), 3

    def call(kernel, out_shape, operands, products, name):
        return pl.pallas_call(
            kernel,
            out_shape=out_shape,
            in_specs=[VMEM] * len(operands),
            out_specs=[VMEM] * len(out_shape),
            compiler_params=LARGE,
            cost_estimate=pl.CostEstimate(
                flops=2 * products * part * part * width,
                bytes_accessed=2 * sum(operand.size for operand in operands),
                transcendentals=products * part * part // 2,
            ),
            name=name,
        )(*operands)

    def tile(rows_of, ready, dtype):
        return call(
            lambda *refs: tile_kernel(rows, rows_of, early if ready else 0, *refs),
            [jax.ShapeDtypeStruct((part, width), dtype)] * len(rows_of),
            [scalars, *[mine[chunk] for chunk in rows_of], *ready, theirs],
            len(rows_of) * (8 - (early if ready else 0)),
            "tile",
        )

    ready = call(
        lambda *refs: weigh_kernel(rows, near, early, *refs),
        [jax.ShapeDtypeStruct((part, early * part), jnp.bfloat16)] * len(near),
        [scalars, *[mine[chunk] for chunk in near], *chunks[:early]],
        len(near) * early,
        "weigh",
    )
    blocks = tile(near, ready, jnp.bfloat16)
    first, second, tail = [
        swap_with(block, neighbour)
        for block, neighbour in zip((blocks[0], blocks[1], blocks[2][size:]), NEIGHBOURS)
    ]
    head = swap_with(blocks[2][:size], NEIGHBOURS[2])
    full = jax.ShapeDtypeStruct((rows, width), jnp.float32)
    column = jax.ShapeDtypeStruct((rows, 1), jnp.float32)
    units = small_call(unit_kernel, [full, full, column, column], [image_emb, text_emb], "units")
    mine[0], units = lax.optimization_barrier((mine[0], units))
    (summed,) = tile((0,), [], jnp.float32)
    (merged,) = small_call(merge_kernel, [spread], [summed, first, second, tail], "merge")
    out = jax.ShapeDtypeStruct((rows, width), jnp.float32)
    own, other = small_call(sum_kernel, [out, out], [exchange(merged), summed, first, second, head], "sum")
    operands = [scalars, own, gather_cores(other), *units]
    return tuple(small_call(finish_kernel, [out, out], operands, "finish"))


def solution(mesh):
    fine = Mesh(mesh.devices.reshape(SHAPE), NAMES)
    return jax.shard_map(
        per_device,
        mesh=fine,
        in_specs=(P(IMG_ORDER, None), P(TXT_ORDER, None), P(), P()),
        out_specs=(P(IMG_ORDER, None), P(TXT_ORDER, None)),
        check_vma=False,
    )
```
